32 devices in a mesh: dp: 8 (over y, x, core), type: 4 (over z).
Axes of the slice: x: 2, y: 2, z: 4, core: 2. Of those that a mesh axis runs over, the one named last changes fastest.
Arguments:
- tokens: bfloat16 [4096, 4096], P(('dp', 'type')), may hold values from -6 to 6
- token_types: int32 [4096, 1], P(('dp', 'type')), may hold values from 0 to 3
- tile_mask: int32 [8, 4, 4], P('dp', 'type'), may hold values from 0 to 1, as said below
- queries: bfloat16 [4096, 4096], P(('dp', 'type')), may hold values from -60 to 60
- keys: bfloat16 [4096, 4096], P(('dp', 'type')), may hold values from -4 to 4
- gate_weight: bfloat16 [4, 4096, 7168], P('type', None, 'dp'), may hold values from -0.09375 to 0.09375
- up_weight: bfloat16 [4, 4096, 7168], P('type', None, 'dp'), may hold values from -0.09375 to 0.09375
- down_weight: bfloat16 [4, 7168, 4096], P('type', 'dp'), may hold values from -0.0625 to 0.0625
Outputs:
- expert_out: bfloat16 [4096, 4096], P(('dp', 'type'))
- attended: bfloat16 [4096, 4096], P(('dp', 'type'))
The draws below stay inside these ranges and needn't reach their ends.
Inputs may be any that keep to these rules, and one draw needn't show every extreme that they name: `tile_mask`: every diagonal entry is 1.
All inputs are finite; a program needn't handle non-finite values.
Results may differ from the reference program's by a relative error of at most 0.02.
Values may be sent and summed in bfloat16 or wider, within the bound.
No kernel may reach another device: no remote copies, remote signals or barrier semaphores. Data moves between devices by JAX's collectives and lax.ppermute only.
A program may use at most 128 MiB of HBM per device.

```python
import math
import jax
import jax.numpy as jnp
from jax import lax

D = 4096
FF = 7168
HEADS = 32
HEAD = 128
TOK_DEV = 128
EXPERTS = 4
SEQ = 512
EVENTS = 8
TOKENS = 4096
EXP_CAP = 16
N_DP = 8
N_TYPE = 4


def query_key_pair(key):
    base = jax.random.fold_in(key, 7)
    query_key, keys_key = jax.random.split(base, 2)
    query_vals = 1.5 * jnp.clip(jax.random.normal(query_key, (TOKENS, D), jnp.float32), -6.0, 6.0)
    key_vals = jnp.clip(jax.random.normal(keys_key, (TOKENS, D), jnp.float32), -4.0, 4.0)
    return (query_vals, key_vals)


def draw_queries(key, part):
    return query_key_pair(key)[0].astype(jnp.bfloat16)


def draw_keys(key, part):
    return query_key_pair(key)[1].astype(jnp.bfloat16)


def draw_tile_mask(key, part):
    random_bits = jax.random.randint(jax.random.fold_in(key, 11), (EVENTS, N_TYPE, N_TYPE), 0, 2, jnp.int32)
    tile_ids = jnp.arange(N_TYPE, dtype=jnp.int32)
    diagonal = (tile_ids[:, None] == tile_ids[None, :]).astype(jnp.int32)
    return jnp.maximum(random_bits, diagonal[None, :, :])


def levels(stream_key, extent, cuts, least, largest):
    factor_of = 1.0
    for axis_at, parts in cuts:
        draws = jax.random.uniform(jax.random.fold_in(jax.random.fold_in(stream_key, 6), axis_at), (parts,), jnp.float32, least / len(cuts), largest / len(cuts))
        factor_of = factor_of * jnp.repeat(jnp.exp(draws), extent[axis_at] // parts).reshape((-1,) + (1,) * (len(extent) - 1 - axis_at))
    return factor_of


def picks_of(own_key, rows, amount, top, lift):
    sequence = jax.random.permutation(jax.random.fold_in(own_key, 1), amount)
    favour = sequence
    for power in range(3):
        favour = favour * favour // amount
    favour = favour * lift // amount
    lots = jax.random.randint(jax.random.fold_in(own_key, 2), (rows, amount), 0, 4096) + favour
    fixed_rows = jax.random.permutation(jax.random.fold_in(own_key, 3), rows)[jnp.arange(amount) % rows]
    lots = jnp.where(jnp.arange(rows)[:, None] == fixed_rows[None, :], 1 << 14, lots)
    priority = lots * amount + jnp.arange(amount)
    return lax.top_k(priority.astype(jnp.int32), top)[1].astype(jnp.int32)


def gaussian(rng, shape, scale, reach, cuts=(), held_as=jnp.bfloat16):
    level = levels(rng, shape, cuts, -0.22, 0.18) if cuts else 1.0
    drawn = jax.random.normal(rng, shape, jnp.float32) * scale * level
    return jnp.minimum(jnp.maximum(drawn, -reach), reach).astype(held_as)


def setup_inputs(seed: int = 0) -> dict:
    streams_of = jax.random.split(jax.random.key(seed), 9)
    return {
        "tokens": gaussian(streams_of[0], (TOKENS, D), 1.0, 6.0, ((0, 32),)),
        "token_types": picks_of(streams_of[1], TOKENS, EXPERTS, 1, 4096),
        "tile_mask": draw_tile_mask(jax.random.fold_in(streams_of[8], 71), 0),
        "queries": draw_queries(jax.random.fold_in(streams_of[8], 71), 0),
        "keys": draw_keys(jax.random.fold_in(streams_of[8], 71), 0),
        "gate_weight": gaussian(streams_of[5], (EXPERTS, D, FF), D ** -0.5, 0.09375, ((0, 4), (2, 8))),
        "up_weight": gaussian(streams_of[6], (EXPERTS, D, FF), D ** -0.5, 0.09375, ((0, 4), (2, 8))),
        "down_weight": gaussian(streams_of[7], (EXPERTS, FF, D), FF ** -0.5, 0.0625, ((0, 4), (1, 8))),
    }


def expert_block(packed_rows, gate_mat, up_mat, down_mat):
    block_width = FF // N_DP

    def accumulate(running, block_index):
        first_col = block_index * block_width
        gate_act = jnp.dot(packed_rows, lax.dynamic_slice_in_dim(gate_mat, first_col, block_width, 1), preferred_element_type=jnp.float32)
        up_act = jnp.dot(packed_rows, lax.dynamic_slice_in_dim(up_mat, first_col, block_width, 1), preferred_element_type=jnp.float32)
        hidden = (jax.nn.silu(gate_act) * up_act).astype(jnp.bfloat16)
        partial_value = jnp.dot(hidden, lax.dynamic_slice_in_dim(down_mat, first_col, block_width, 0), preferred_element_type=jnp.float32).astype(jnp.bfloat16)
        return (running + partial_value.astype(jnp.float32), None)
    combined, _ = lax.scan(accumulate, jnp.zeros((packed_rows.shape[0], D), jnp.float32), jnp.arange(N_DP, dtype=jnp.int32))
    return combined.astype(jnp.bfloat16)

def attend(query_rows, key_rows, value_rows, allowed):
    query_heads = query_rows.astype(jnp.float32).reshape(SEQ, HEADS, HEAD)
    key_heads = key_rows.astype(jnp.float32).reshape(SEQ, HEADS, HEAD)
    value_heads = value_rows.astype(jnp.float32).reshape(SEQ, HEADS, HEAD)
    scores = jnp.einsum('qhd,khd->hqk', query_heads, key_heads) * (1.0 / math.sqrt(HEAD))
    masked = jnp.where(allowed[None], scores, -jnp.inf)
    row_max = lax.optimization_barrier(jnp.max(masked, axis=-1, keepdims=True))
    weights = jnp.where(allowed[None], jnp.exp(masked - row_max), 0.0).astype(jnp.bfloat16)
    total_weight = lax.optimization_barrier(jnp.sum(weights.astype(jnp.float32), axis=-1))
    mixed_rows = jnp.einsum('hqk,khd->qhd', weights.astype(jnp.float32), value_heads) / jnp.transpose(total_weight)[:, :, None]
    return mixed_rows.reshape(SEQ, D).astype(jnp.bfloat16)

def reference(tokens, token_types, tile_mask, queries, keys, gate_weight, up_weight, down_weight):
    flat_types = token_types[:, 0].astype(jnp.int32)
    type_grid = flat_types.reshape(EVENTS, SEQ)
    one_hot = (type_grid[:, :, None] == jnp.arange(EXPERTS, dtype=jnp.int32)[None, None, :]).astype(jnp.int32)
    event_rank = lax.optimization_barrier(jnp.sum((jnp.cumsum(one_hot, axis=1, dtype=jnp.int32) - one_hot) * one_hot, axis=2, dtype=jnp.int32))
    slot_grid = jnp.arange(EVENTS, dtype=jnp.int32)[:, None] * EXP_CAP + event_rank
    slot_grid = jnp.where(event_rank < EXP_CAP, slot_grid, EVENTS * EXP_CAP)
    slot_index = slot_grid.reshape(TOKENS).astype(jnp.int32)
    packed = jnp.zeros((EXPERTS, EVENTS * EXP_CAP, D), jnp.bfloat16).at[flat_types, slot_index].set(tokens, mode='drop')
    expert_packed = lax.map(lambda packed_args: expert_block(*packed_args), (packed, gate_weight, up_weight, down_weight))
    expert_out = expert_packed.at[flat_types, slot_index].get(mode='fill', fill_value=0)
    tile_index = jnp.arange(SEQ, dtype=jnp.int32) // TOK_DEV

    def per_event(event_args):
        query_rows, key_rows, value_rows, mask_rows = event_args
        allowed = mask_rows[tile_index[:, None], tile_index[None, :]] == 1
        return attend(query_rows, key_rows, value_rows, allowed)
    attended = lax.map(per_event, (queries.reshape(EVENTS, SEQ, D), keys.reshape(EVENTS, SEQ, D), expert_out.reshape(EVENTS, SEQ, D), tile_mask))
    return (expert_out, attended.reshape(TOKENS, D))
```

```python
import functools
import math

import jax
import jax.numpy as jnp
from jax import lax
from jax.experimental import pallas as pl
from jax.experimental.pallas import tpu as pltpu
from jax.sharding import PartitionSpec as P

HEAD = 128
EXP_CAP = 16
LANES = 128
MASKED = -1e30
VMEM_BYTES = 56 * 1024 * 1024
VMEM = pl.BlockSpec(memory_space=pltpu.VMEM)


def params(**more):
    return pltpu.CompilerParams(vmem_limit_bytes=VMEM_BYTES, **more)


def cost(flops, bytes_accessed, transcendentals=0):
    return pl.CostEstimate(
        flops=int(flops), bytes_accessed=int(bytes_accessed), transcendentals=int(transcendentals)
    )


def strict_upper(size):
    earlier = lax.broadcasted_iota(jnp.int32, (size, size), 0)
    later = lax.broadcasted_iota(jnp.int32, (size, size), 1)
    return (earlier < later).astype(jnp.bfloat16)


def columns(width):
    for chunk in (1024, 512, 256, 128):
        if width % chunk == 0:
            return chunk, width // chunk
    raise ValueError(width)


def route_kernel(n_type, types_ref, mask_ref, tokens_ref, *out_refs):
    me = lax.axis_index("type")
    rows, width = tokens_ref.shape
    types = types_ref[...]
    type_rows = 2 * 8
    hot = lax.broadcasted_iota(jnp.int32, (type_rows, rows), 0) == types
    before = jnp.dot(
        hot.astype(jnp.bfloat16), strict_upper(rows), preferred_element_type=jnp.float32
    )
    rank = jnp.sum(jnp.where(hot, before, 0.0), axis=0, keepdims=True).astype(jnp.int32)
    place = jnp.where(rank < EXP_CAP, jnp.bitwise_xor(types, me) * EXP_CAP + rank, -1)
    select = (
        lax.broadcasted_iota(jnp.int32, (n_type * EXP_CAP, rows), 0) == place
    ).astype(jnp.bfloat16)
    chunk, count = columns(width)
    for c in range(count):
        span = pl.ds(c * chunk, chunk)
        moved = jnp.dot(select, tokens_ref[:, span], preferred_element_type=jnp.float32).astype(
            jnp.bfloat16
        )
        for s in range(n_type):
            out_refs[s][:, span] = moved[s * EXP_CAP : (s + 1) * EXP_CAP]
    lane = lax.broadcasted_iota(jnp.int32, (EXP_CAP, LANES), 1)
    row = lax.broadcasted_iota(jnp.int32, (EXP_CAP, LANES), 0)
    mask_row = jnp.zeros((EXP_CAP, LANES), jnp.int32)
    for j in range(n_type):
        mask_row = jnp.where(lane == j, mask_ref[0, j], mask_row)
    extra = jnp.where(row == 0, types, jnp.where(row == 1, mask_row, 0))
    extra = extra.astype(jnp.float32).astype(jnp.bfloat16)
    for s in range(n_type):
        out_refs[s][:, pl.ds(width, LANES)] = extra


def route(n_type, types, mask_row, tokens):
    rows, width = tokens.shape
    wide = width + LANES
    return pl.pallas_call(
        functools.partial(route_kernel, n_type),
        out_shape=[jax.ShapeDtypeStruct((EXP_CAP, wide), jnp.bfloat16)] * n_type,
        in_specs=[VMEM, pl.BlockSpec(memory_space=pltpu.SMEM), VMEM],
        out_specs=[VMEM] * n_type,
        compiler_params=params(),
        cost_estimate=cost(2 * n_type * EXP_CAP * rows * width, 2 * rows * width * 2),
    )(types, mask_row, tokens)


def pack_kernel(n_type, *refs):
    in_refs, packed_ref, info_ref = refs[:n_type], refs[n_type], refs[n_type + 1]
    me = lax.axis_index("type")
    width = packed_ref.shape[1]
    tail = pl.ds(width, LANES)
    type_rows = 2 * 8
    row = lax.broadcasted_iota(jnp.int32, (type_rows, LANES), 0)
    upper = strict_upper(LANES)
    extras = [ref[:, tail].astype(jnp.float32) for ref in in_refs]
    types = [e[0:1] for e in extras]
    hots = [row == t.astype(jnp.int32) for t in types]
    befores = [
        jnp.dot(h.astype(jnp.bfloat16), upper, preferred_element_type=jnp.float32) for h in hots
    ]
    counts = [jnp.sum(h.astype(jnp.float32), axis=1, keepdims=True) for h in hots]
    lane16 = lax.broadcasted_iota(jnp.int32, (EXP_CAP, n_type * EXP_CAP), 1)
    slot16 = lax.broadcasted_iota(jnp.int32, (EXP_CAP, n_type * EXP_CAP), 0)
    compact = jnp.zeros((EXP_CAP, n_type * EXP_CAP), jnp.bool_)
    mine = lax.broadcasted_iota(jnp.int32, (type_rows, 1), 0) == me
    info_rows = []
    for s in range(n_type):
        ahead = jnp.zeros((type_rows, 1), jnp.float32)
        for other in range(n_type):
            if other != s:
                first = jnp.bitwise_xor(me, other) < jnp.bitwise_xor(me, s)
                ahead = ahead + jnp.where(first, counts[other], 0.0)
        rank = jnp.sum(jnp.where(hots[s], befores[s] + ahead, 0.0), axis=0, keepdims=True)
        info_rows.append(jnp.where(rank < EXP_CAP, types[s] * EXP_CAP + rank, -1.0))
        offset = jnp.sum(jnp.where(mine, ahead, 0.0)).astype(jnp.int32)
        amount = jnp.sum(jnp.where(mine, counts[s], 0.0)).astype(jnp.int32)
        local = lane16 - s * EXP_CAP
        compact = compact | (
            (local >= 0) & (local < EXP_CAP) & (local < amount) & (local + offset == slot16)
        )
    lane = lax.broadcasted_iota(jnp.int32, (1, LANES), 1)
    for q in range(2):
        for s in range(n_type):
            kept = jnp.sum(
                jnp.where(lane == jnp.bitwise_xor(me, s), extras[q][1:2], 0.0),
                axis=1,
                keepdims=True,
            )
            info_rows.append(jnp.broadcast_to(jnp.where(kept == 1.0, 0.0, MASKED), (1, LANES)))
    for at, info_row in enumerate(info_rows):
        info_ref[at : at + 1, :] = info_row
    compact = compact.astype(jnp.bfloat16)
    chunk, count = columns(width)
    for c in range(count):
        span = pl.ds(c * chunk, chunk)
        rows = jnp.concatenate([ref[:, span] for ref in in_refs], axis=0)
        packed_ref[:, span] = jnp.dot(compact, rows, preferred_element_type=jnp.float32).astype(
            jnp.bfloat16
        )


def pack(n_type, incoming):
    width = incoming[0].shape[1] - LANES
    return pl.pallas_call(
        functools.partial(pack_kernel, n_type),
        out_shape=[
            jax.ShapeDtypeStruct((EXP_CAP, width), jnp.bfloat16),
            jax.ShapeDtypeStruct((3 * n_type, LANES), jnp.float32),
        ],
        in_specs=[VMEM] * n_type,
        out_specs=[VMEM, VMEM],
        compiler_params=params(),
        cost_estimate=cost(2 * n_type * EXP_CAP * EXP_CAP * width, 6 * EXP_CAP * width * 2),
    )(*incoming)


def ffn_kernel(steps, near_ref, far_ref, gate_ref, up_ref, down_ref, own_ref, away_ref, x_ref, gate_acc, up_acc, hidden_ref):
    step = pl.program_id(0)
    half = near_ref.shape[0]
    depth = gate_ref.shape[0]

    @pl.when(step == 0)
    def _():
        x_ref[:half] = near_ref[...]
        x_ref[half:] = far_ref[...]

    @pl.when(step < steps)
    def _():
        x = x_ref[:, pl.ds(pl.multiple_of(step * depth, depth), depth)]
        gate = jnp.dot(x, gate_ref[...], preferred_element_type=jnp.float32)
        up = jnp.dot(x, up_ref[...], preferred_element_type=jnp.float32)

        @pl.when(step == 0)
        def _():
            gate_acc[...] = gate
            up_acc[...] = up

        @pl.when(step > 0)
        def _():
            gate_acc[...] += gate
            up_acc[...] += up

    @pl.when(step == steps - 1)
    def _():
        gate = gate_acc[...]
        hidden_ref[...] = (gate / (1.0 + jnp.exp(-gate)) * up_acc[...]).astype(jnp.bfloat16)

    @pl.when(step >= steps)
    def _():
        out = jnp.dot(hidden_ref[...], down_ref[...], preferred_element_type=jnp.float32)
        own_ref[...] = out[:half]
        away_ref[...] = out[half:].astype(jnp.bfloat16)


def ffn(near, far, gate, up, down):
    half, width = near.shape
    rows = 2 * half
    hidden = gate.shape[1]
    depth, steps = columns(width)
    depth, steps = 512, width // 512
    first = lambda i: (jnp.minimum(i, steps - 1), 0)
    second = lambda i: (0, jnp.maximum(i - steps, 0))
    return pl.pallas_call(
        functools.partial(ffn_kernel, steps),
        grid=(2 * steps,),
        out_shape=[
            jax.ShapeDtypeStruct((half, width), jnp.float32),
            jax.ShapeDtypeStruct((half, width), jnp.bfloat16),
        ],
        in_specs=[
            VMEM,
            VMEM,
            pl.BlockSpec((depth, hidden), first),
            pl.BlockSpec((depth, hidden), first),
            pl.BlockSpec((hidden, depth), second),
        ],
        out_specs=[pl.BlockSpec((half, depth), second), pl.BlockSpec((half, depth), second)],
        scratch_shapes=[
            pltpu.VMEM((rows, width), jnp.bfloat16),
            pltpu.VMEM((rows, hidden), jnp.float32),
            pltpu.VMEM((rows, hidden), jnp.float32),
            pltpu.VMEM((rows, hidden), jnp.bfloat16),
        ],
        compiler_params=params(dimension_semantics=("arbitrary",)),
        cost_estimate=cost(6 * rows * width * hidden, 6 * width * hidden, rows * hidden),
    )(near, far, gate, up, down)


def weigh_kernel(n_type, n_query, info_ref, *refs):
    query_refs = refs[:n_query]
    key_refs = refs[n_query : n_query + n_type]
    out_refs = refs[n_query + n_type : 2 * n_query + n_type]
    select_ref = refs[-1]
    slots = n_type * EXP_CAP
    tile = key_refs[0].shape[0]

    @pl.when(pl.program_id(0) == 0)
    def _():
        row = lax.broadcasted_iota(jnp.int32, (slots + 2 * 8, tile), 0)
        for s in range(n_type):
            slot = info_ref[s : s + 1, :].astype(jnp.int32)
            select_ref[:, s * tile : (s + 1) * tile] = ((row == slot) | (row == slots)).astype(
                jnp.bfloat16
            )

    select = select_ref[...]
    scale = 1.0 / math.sqrt(HEAD)
    bias = []
    for s in range(n_type):
        rows = [info_ref[(1 + q) * n_type + s : (1 + q) * n_type + s + 1, :] for q in range(n_query)]
        bias.append(jnp.concatenate(rows, axis=1) if n_query > 1 else rows[0])
    for h in range(out_refs[0].shape[0]):
        span = pl.ds(h * HEAD, HEAD)
        query = jnp.concatenate([ref[:, span] for ref in query_refs], axis=0)
        scores = [
            lax.dot_general(
                ref[:, span], query, (((1,), (1,)), ((), ())), preferred_element_type=jnp.float32
            )
            * scale
            + bias[s]
            for s, ref in enumerate(key_refs)
        ]
        scores = jnp.concatenate(scores, axis=0)
        top = jnp.max(scores, axis=0, keepdims=True)
        weights = jnp.exp(scores - top).astype(jnp.bfloat16)
        picked = jnp.dot(select, weights, preferred_element_type=jnp.float32)
        normal = (picked[:slots] / picked[slots : slots + 1]).astype(jnp.bfloat16)
        for q in range(n_query):
            out_refs[q][h] = normal[:, q * tile : (q + 1) * tile]


def weigh(n_type, info, queries, keys, per_step=4):
    tile, width = keys[0].shape
    heads = width // HEAD
    n_query = len(queries)
    slots = n_type * EXP_CAP
    block = pl.BlockSpec((tile, per_step * HEAD), lambda i: (0, i))
    out_block = pl.BlockSpec((per_step, slots, tile), lambda i: (i, 0, 0))
    return pl.pallas_call(
        functools.partial(weigh_kernel, n_type, n_query),
        grid=(heads // per_step,),
        out_shape=[jax.ShapeDtypeStruct((heads, slots, tile), jnp.bfloat16)] * n_query,
        in_specs=[VMEM] + [block] * (n_query + n_type),
        out_specs=[out_block] * n_query,
        scratch_shapes=[pltpu.VMEM((slots + 2 * 8, n_type * tile), jnp.bfloat16)],
        compiler_params=params(dimension_semantics=("arbitrary",)),
        cost_estimate=cost(
            4 * n_query * tile * n_type * tile * width,
            2 * (n_query + n_type) * tile * width,
            n_query * tile * n_type * tile * heads,
        ),
    )(info, *queries, *keys)


def finish_kernel(n_type, n_part, info_ref, *refs):
    own_refs, back_refs = refs[:n_part], refs[n_part : 2 * n_part]
    value_refs = refs[2 * n_part : 2 * n_part + n_type]
    out_ref, attended_ref, value_ref = refs[2 * n_part + n_type :]
    me = lax.axis_index("type")
    ends = (me == 0) | (me == n_type - 1)
    tile = out_ref.shape[0]
    width = out_ref.shape[1]
    for s in range(n_type):
        at = pl.multiple_of(jnp.bitwise_xor(me, s) * EXP_CAP, EXP_CAP)
        value_ref[pl.ds(at, EXP_CAP), :] = value_refs[s][...]
    row = lax.broadcasted_iota(jnp.int32, (n_type * EXP_CAP, tile), 0)
    select = (row == info_ref[0:1, :].astype(jnp.int32)).astype(jnp.bfloat16)
    chunk, count = columns(width)
    contract = (((0,), (0,)), ((), ()))
    for c in range(count):
        span = pl.ds(c * chunk, chunk)
        out_ref[:, span] = lax.dot_general(
            select, value_ref[:, span], contract, preferred_element_type=jnp.float32
        ).astype(jnp.bfloat16)
    at = 0
    for part in range(n_part):
        for h in range(own_refs[part].shape[0]):
            span = pl.ds(at * HEAD, HEAD)
            weights = own_refs[part][h]
            if back_refs:
                weights = jnp.where(ends, back_refs[part][h], weights)
            attended_ref[:, span] = lax.dot_general(
                weights, value_ref[:, span], contract, preferred_element_type=jnp.float32
            ).astype(jnp.bfloat16)
            at += 1


def finish(n_type, info, own, back, values, tile):
    width = values[0].shape[1]
    n_part = len(own)
    return pl.pallas_call(
        functools.partial(finish_kernel, n_type, n_part),
        out_shape=[jax.ShapeDtypeStruct((tile, width), jnp.bfloat16)] * 2,
        in_specs=[VMEM] * (1 + 2 * n_part + n_type),
        out_specs=[VMEM] * 2,
        scratch_shapes=[pltpu.VMEM((n_type * EXP_CAP, width), jnp.bfloat16)],
        compiler_params=params(),
        cost_estimate=cost(4 * tile * n_type * EXP_CAP * width, 6 * tile * width),
    )(info, *own, *back, *values)


def swap(x, axis, size, s):
    return lax.ppermute(x, axis, [(i, i ^ s) for i in range(size)])


def on_device(n_dp, n_type, tokens, token_types, tile_mask, queries, keys, gate_weight, up_weight, down_weight):
    tile, width = tokens.shape
    outgoing = route(n_type, token_types.reshape(1, tile), tile_mask.reshape(1, n_type), tokens)
    incoming = [outgoing[0]] + [swap(outgoing[s], "type", n_type, s) for s in range(1, n_type)]
    packed, info = pack(n_type, incoming)

    if n_type == 4:
        packed, info, keys, queries = lax.optimization_barrier((packed, info, keys, queries))
        n_part = 2
        to_middle = [(0, 1), (3, 2)]
        across = [(1, 2), (2, 1)]
        to_end = [(1, 0), (2, 3)]
        wide = width // n_part
        own_weights, back_weights = [], []
        for part in range(n_part):
            span = slice(part * wide, (part + 1) * wide)
            key_part, query_part = keys[:, span], queries[:, span]
            near = lax.ppermute(key_part, "type", to_middle)
            other = lax.ppermute(key_part, "type", across)
            far = lax.ppermute(near, "type", across)
            guest = lax.ppermute(query_part, "type", to_middle)
            own, theirs = weigh(n_type, info, [query_part, guest], [key_part, near, far, other])
            own_weights.append(own)
            back_weights.append(lax.ppermute(theirs, "type", to_end))
    else:
        others = [keys] + [swap(keys, "type", n_type, s) for s in range(1, n_type)]
        own_weights = list(weigh(n_type, info, [queries], others))
        back_weights = own_weights

    n_same = n_dp // 2
    same_core = jnp.concatenate(
        [packed] + [swap(packed, "dp", n_dp, 2 * p) for p in range(1, n_same)], axis=0
    )
    other_core = swap(same_core, "dp", n_dp, 1)
    own_rows, away_rows = ffn(same_core, other_core, gate_weight[0], up_weight[0], down_weight[0])
    from_core = swap(away_rows, "dp", n_dp, 1)
    chip_rows = (own_rows + from_core.astype(jnp.float32)).astype(jnp.bfloat16)
    pieces = [chip_rows[p * EXP_CAP : (p + 1) * EXP_CAP] for p in range(n_same)]
    total = pieces[0].astype(jnp.float32)
    for p in range(1, n_same):
        total = total + swap(pieces[p], "dp", n_dp, 2 * p).astype(jnp.float32)
    expert_rows = total.astype(jnp.bfloat16)
    values = [expert_rows] + [swap(expert_rows, "type", n_type, s) for s in range(1, n_type)]
    expert_out, attended = finish(n_type, info, own_weights, back_weights, values, tile)
    return (expert_out, attended)


def solution(mesh):
    return jax.shard_map(
        functools.partial(on_device, mesh.shape["dp"], mesh.shape["type"]),
        mesh=mesh,
        in_specs=(
            P(("dp", "type"), None),
            P(("dp", "type"), None),
            P("dp", "type", None),
            P(("dp", "type"), None),
            P(("dp", "type"), None),
            P("type", None, "dp"),
            P("type", None, "dp"),
            P("type", "dp", None),
        ),
        out_specs=(P(("dp", "type"), None), P(("dp", "type"), None)),
        check_vma=False,
    )
```

```python
import functools
import math

import jax
import jax.numpy as jnp
from jax import lax
from jax.experimental import pallas as pl
from jax.experimental.pallas import tpu as pltpu
from jax.sharding import PartitionSpec as P

HEAD = 128
EXP_CAP = 16
LANES = 128
MASKED = -1e30
MIB = 1024 * 1024
VMEM = pl.BlockSpec(memory_space=pltpu.VMEM)


def params(mib, **more):
    return pltpu.CompilerParams(vmem_limit_bytes=mib * MIB, **more)


def held(arrays):
    return [pltpu.with_memory_space_constraint(x, pltpu.VMEM) for x in arrays]


def cost(flops, bytes_accessed, transcendentals=0):
    return pl.CostEstimate(
        flops=int(flops), bytes_accessed=int(bytes_accessed), transcendentals=int(transcendentals)
    )


def strict_upper(size):
    earlier = lax.broadcasted_iota(jnp.int32, (size, size), 0)
    later = lax.broadcasted_iota(jnp.int32, (size, size), 1)
    return (earlier < later).astype(jnp.bfloat16)


def columns(width):
    for chunk in (1024, 512, 256, 128):
        if width % chunk == 0:
            return chunk, width // chunk
    raise ValueError(width)


def route_kernel(n_type, types_ref, mask_ref, tokens_ref, *refs):
    out_refs, select_ref = refs[:n_type], refs[n_type]
    me = lax.axis_index("type")
    step = pl.program_id(0)
    rows, chunk = tokens_ref.shape
    width = out_refs[0].shape[1] - LANES

    @pl.when(step == 0)
    def _():
        types = types_ref[...]
        hot = lax.broadcasted_iota(jnp.int32, (EXP_CAP, rows), 0) == types
        before = jnp.dot(
            hot.astype(jnp.bfloat16), strict_upper(rows), preferred_element_type=jnp.float32
        )
        rank = jnp.sum(jnp.where(hot, before, 0.0), axis=0, keepdims=True).astype(jnp.int32)
        place = jnp.where(rank < EXP_CAP, jnp.bitwise_xor(types, me) * EXP_CAP + rank, -1)
        select_ref[...] = (
            lax.broadcasted_iota(jnp.int32, (n_type * EXP_CAP, rows), 0) == place
        ).astype(jnp.bfloat16)
        lane = lax.broadcasted_iota(jnp.int32, (EXP_CAP, LANES), 1)
        row = lax.broadcasted_iota(jnp.int32, (EXP_CAP, LANES), 0)
        mask_row = jnp.zeros((EXP_CAP, LANES), jnp.int32)
        for j in range(n_type):
            mask_row = jnp.where(lane == j, mask_ref[0, j], mask_row)
        extra = jnp.where(row == 0, types, jnp.where(row == 1, mask_row, 0))
        extra = extra.astype(jnp.float32).astype(jnp.bfloat16)
        for s in range(n_type):
            out_refs[s][:, pl.ds(width, LANES)] = extra

    moved = jnp.dot(select_ref[...], tokens_ref[...], preferred_element_type=jnp.float32).astype(
        jnp.bfloat16
    )
    span = pl.ds(pl.multiple_of(step * chunk, chunk), chunk)
    for s in range(n_type):
        out_refs[s][:, span] = moved[s * EXP_CAP : (s + 1) * EXP_CAP]


def route(n_type, types, mask_row, tokens):
    rows, width = tokens.shape
    wide = width + LANES
    chunk, count = columns(width)
    return pl.pallas_call(
        functools.partial(route_kernel, n_type),
        grid=(count,),
        out_shape=[jax.ShapeDtypeStruct((EXP_CAP, wide), jnp.bfloat16)] * n_type,
        in_specs=[
            VMEM,
            pl.BlockSpec(memory_space=pltpu.SMEM),
            pl.BlockSpec((rows, chunk), lambda i: (0, i)),
        ],
        out_specs=[VMEM] * n_type,
        scratch_shapes=[pltpu.VMEM((n_type * EXP_CAP, rows), jnp.bfloat16)],
        compiler_params=params(8, dimension_semantics=("arbitrary",)),
        cost_estimate=cost(0, 0),
    )(*[pltpu.with_memory_space_constraint(x, pltpu.HBM) for x in (types, mask_row, tokens)])


def fetch_kernel(count, *refs):
    sems = refs[2 * count]
    copies = [pltpu.make_async_copy(refs[i], refs[count + i], sems.at[i]) for i in range(count)]
    for copy in copies:
        copy.start()
    for copy in copies:
        copy.wait()


def fetch(arrays):
    count = len(arrays)
    return pl.pallas_call(
        functools.partial(fetch_kernel, count),
        out_shape=[pltpu.VMEM(x.shape, x.dtype) for x in arrays],
        in_specs=[pl.BlockSpec(memory_space=pl.ANY)] * count,
        out_specs=[VMEM] * count,
        scratch_shapes=[pltpu.SemaphoreType.DMA((count,))],
        compiler_params=params(1),
        cost_estimate=cost(0, 2 * sum(x.size * 2 for x in arrays)),
    )(*[pltpu.with_memory_space_constraint(x, pltpu.HBM) for x in arrays])


def pack_kernel(n_type, *refs):
    in_refs, packed_ref, info_ref = refs[:n_type], refs[n_type], refs[n_type + 1]
    me = lax.axis_index("type")
    width = packed_ref.shape[1]
    tail = pl.ds(width, LANES)
    type_rows = 2 * 8
    row = lax.broadcasted_iota(jnp.int32, (type_rows, LANES), 0)
    upper = strict_upper(LANES)
    extras = [ref[:, tail].astype(jnp.float32) for ref in in_refs]
    types = [e[0:1] for e in extras]
    hots = [row == t.astype(jnp.int32) for t in types]
    befores = [
        jnp.dot(h.astype(jnp.bfloat16), upper, preferred_element_type=jnp.float32) for h in hots
    ]
    counts = [jnp.sum(h.astype(jnp.float32), axis=1, keepdims=True) for h in hots]
    lane16 = lax.broadcasted_iota(jnp.int32, (EXP_CAP, n_type * EXP_CAP), 1)
    slot16 = lax.broadcasted_iota(jnp.int32, (EXP_CAP, n_type * EXP_CAP), 0)
    compact = jnp.zeros((EXP_CAP, n_type * EXP_CAP), jnp.bool_)
    mine = lax.broadcasted_iota(jnp.int32, (type_rows, 1), 0) == me
    info_rows = []
    for s in range(n_type):
        ahead = jnp.zeros((type_rows, 1), jnp.float32)
        for other in range(n_type):
            if other != s:
                first = jnp.bitwise_xor(me, other) < jnp.bitwise_xor(me, s)
                ahead = ahead + jnp.where(first, counts[other], 0.0)
        rank = jnp.sum(jnp.where(hots[s], befores[s] + ahead, 0.0), axis=0, keepdims=True)
        info_rows.append(jnp.where(rank < EXP_CAP, types[s] * EXP_CAP + rank, -1.0))
        offset = jnp.sum(jnp.where(mine, ahead, 0.0)).astype(jnp.int32)
        amount = jnp.sum(jnp.where(mine, counts[s], 0.0)).astype(jnp.int32)
        local = lane16 - s * EXP_CAP
        compact = compact | (
            (local >= 0) & (local < EXP_CAP) & (local < amount) & (local + offset == slot16)
        )
    lane = lax.broadcasted_iota(jnp.int32, (1, LANES), 1)
    for q in range(2):
        for s in range(n_type):
            kept = jnp.sum(
                jnp.where(lane == jnp.bitwise_xor(me, s), extras[q][1:2], 0.0),
                axis=1,
                keepdims=True,
            )
            info_rows.append(jnp.broadcast_to(jnp.where(kept == 1.0, 0.0, MASKED), (1, LANES)))
    for at, info_row in enumerate(info_rows):
        info_ref[at : at + 1, :] = info_row
    compact = compact.astype(jnp.bfloat16)
    chunk, count = columns(width)
    for c in range(count):
        span = pl.ds(c * chunk, chunk)
        rows = jnp.concatenate([ref[:, span] for ref in in_refs], axis=0)
        packed_ref[:, span] = jnp.dot(compact, rows, preferred_element_type=jnp.float32).astype(
            jnp.bfloat16
        )


def pack(n_type, incoming):
    width = incoming[0].shape[1] - LANES
    return pl.pallas_call(
        functools.partial(pack_kernel, n_type),
        out_shape=[
            jax.ShapeDtypeStruct((EXP_CAP, width), jnp.bfloat16),
            jax.ShapeDtypeStruct((3 * n_type, LANES), jnp.float32),
        ],
        in_specs=[VMEM] * n_type,
        out_specs=[VMEM, VMEM],
        compiler_params=params(8),
        cost_estimate=cost(0, 0),
    )(*held(incoming))


def ffn_kernel(near_ref, far_ref, gate_ref, up_ref, down_ref, own_ref, away_ref, x_ref, hidden_ref):
    half = near_ref.shape[0]
    x_ref[:half] = near_ref[...]
    x_ref[half:] = far_ref[...]
    hidden = gate_ref.shape[1]
    for at in range(0, hidden, 256):
        span = pl.ds(at, min(256, hidden - at))
        gate = jnp.dot(x_ref[...], gate_ref[:, span], preferred_element_type=jnp.float32)
        up = jnp.dot(x_ref[...], up_ref[:, span], preferred_element_type=jnp.float32)
        hidden_ref[:, span] = (gate / (1.0 + jnp.exp(-gate)) * up).astype(jnp.bfloat16)
    for at in range(0, down_ref.shape[1], 512):
        span = pl.ds(at, 512)
        out = jnp.dot(hidden_ref[...], down_ref[:, span], preferred_element_type=jnp.float32)
        own_ref[:, span] = out[:half]
        away_ref[:, span] = out[half:].astype(jnp.bfloat16)


def ffn(near, far, gate, up, down):
    half, width = near.shape
    rows = 2 * half
    hidden = gate.shape[1]
    return pl.pallas_call(
        ffn_kernel,
        out_shape=[
            jax.ShapeDtypeStruct((half, width), jnp.float32),
            jax.ShapeDtypeStruct((half, width), jnp.bfloat16),
        ],
        in_specs=[VMEM] * 5,
        out_specs=[VMEM] * 2,
        scratch_shapes=[
            pltpu.VMEM((rows, width), jnp.bfloat16),
            pltpu.VMEM((rows, hidden), jnp.bfloat16),
        ],
        compiler_params=params(16),
        cost_estimate=cost(0, 0),
    )(*held([near, far, gate, up, down]))


def weigh_setup(n_type, tile_ids, query_ids, info_ref, select_ref, mask_ref, pick_ref):
    slots = n_type * EXP_CAP
    tile = select_ref.shape[1] // len(tile_ids)
    row = lax.broadcasted_iota(jnp.int32, (slots + 2 * 8, tile), 0)
    lane = lax.broadcasted_iota(jnp.int32, (tile, HEAD), 1)
    for at, s in enumerate(tile_ids):
        slot = info_ref[s : s + 1, :].astype(jnp.int32)
        select_ref[:, at * tile : (at + 1) * tile] = ((row == slot) | (row == slots)).astype(
            jnp.bfloat16
        )
        mask = jnp.zeros((tile, HEAD), jnp.float32)
        for q in query_ids:
            line = (1 + q) * n_type + s
            mask = jnp.where(lane == q, info_ref[line : line + 1, :], mask)
        mask_ref[at * tile : (at + 1) * tile, :] = mask.astype(jnp.bfloat16)
    for at, q in enumerate(query_ids):
        pick_ref[at * tile : (at + 1) * tile, :] = (lane == q).astype(jnp.bfloat16)


def weigh_scores(keys, queries, mask_ref, pick_ref):
    return lax.dot_general(
        jnp.concatenate([jnp.concatenate(keys, axis=0), mask_ref[...]], axis=1),
        jnp.concatenate([jnp.concatenate(queries, axis=0), pick_ref[...]], axis=1),
        (((1,), (1,)), ((), ())),
        preferred_element_type=jnp.float32,
    )


FACTOR = math.log2(math.e) / math.sqrt(HEAD)


def weigh_begin_kernel(n_type, tile_ids, query_id, info_ref, query_ref, *refs):
    key_refs = refs[: len(tile_ids)]
    state_ref, select_ref, mask_ref, pick_ref = refs[len(tile_ids) :]
    weigh_setup(n_type, tile_ids, [query_id], info_ref, select_ref, mask_ref, pick_ref)
    rows = n_type * EXP_CAP + 8
    tile = query_ref.shape[0]

    def body(h, carry):
        span = pl.ds(pl.multiple_of(h * HEAD, HEAD), HEAD)
        scores = weigh_scores(
            [ref[:, span] for ref in key_refs], [query_ref[:, span]], mask_ref, pick_ref
        )
        top = jnp.max(scores, axis=0, keepdims=True)
        weights = jnp.exp2((scores - top) * FACTOR).astype(jnp.bfloat16)
        picked = jnp.dot(select_ref[...], weights, preferred_element_type=jnp.float32)
        state_ref[h, :rows] = picked[:rows]
        state_ref[h, rows:] = jnp.broadcast_to(top, (8, tile))
        return carry

    lax.fori_loop(0, state_ref.shape[0], body, 0, unroll=4)


def weigh_scratch(n_type, n_tile, n_query, tile):
    return [
        pltpu.VMEM((n_type * EXP_CAP + 2 * 8, n_tile * tile), jnp.bfloat16),
        pltpu.VMEM((n_tile * tile, HEAD), jnp.bfloat16),
        pltpu.VMEM((n_query * tile, HEAD), jnp.bfloat16),
    ]


def weigh_begin(n_type, info, query, query_id, keys, tile_ids):
    tile, width = query.shape
    heads = width // HEAD
    return pl.pallas_call(
        functools.partial(weigh_begin_kernel, n_type, tile_ids, query_id),
        out_shape=jax.ShapeDtypeStruct((heads, n_type * EXP_CAP + 2 * 8, tile), jnp.float32),
        in_specs=[VMEM] * (2 + len(keys)),
        out_specs=VMEM,
        scratch_shapes=weigh_scratch(n_type, len(keys), 1, tile),
        compiler_params=params(8),
        cost_estimate=cost(0, 16 * tile * tile * heads),
    )(*held([info, query, *keys]))


def weigh_end_kernel(n_type, tile_id, first_head, info_ref, key_ref, *refs):
    n_query = (len(refs) - 3) // 3
    query_refs, state_refs = refs[:n_query], refs[n_query : 2 * n_query]
    out_refs = refs[2 * n_query : 3 * n_query]
    select_ref, mask_ref, pick_ref = refs[3 * n_query :]
    weigh_setup(n_type, [tile_id], range(n_query), info_ref, select_ref, mask_ref, pick_ref)
    slots = n_type * EXP_CAP
    rows = slots + 8
    tile = key_ref.shape[0]

    def body(h, carry):
        head = h + first_head
        span = pl.ds(pl.multiple_of(head * HEAD, HEAD), HEAD)
        scores = weigh_scores(
            [key_ref[:, span]], [ref[:, span] for ref in query_refs], mask_ref, pick_ref
        )
        before = jnp.concatenate([ref[head, rows : rows + 1] for ref in state_refs], axis=1)
        top = jnp.maximum(before, jnp.max(scores, axis=0, keepdims=True))
        weights = jnp.exp2((scores - top) * FACTOR).astype(jnp.bfloat16)
        picked = jnp.dot(select_ref[...], weights, preferred_element_type=jnp.float32)[:rows]
        shrink = jnp.exp2((before - top) * FACTOR)
        for q in range(n_query):
            mine = slice(q * tile, (q + 1) * tile)
            total = state_refs[q][head, :rows] * shrink[:, mine] + picked[:, mine]
            out_refs[q][h] = (total[:slots] * (1.0 / total[slots : slots + 1])).astype(jnp.bfloat16)
        return carry

    lax.fori_loop(0, out_refs[0].shape[0], body, 0, unroll=4)


def weigh_end(n_type, info, key, tile_id, queries, states, first_head, heads):
    tile = key.shape[0]
    n_query = len(queries)
    return pl.pallas_call(
        functools.partial(weigh_end_kernel, n_type, tile_id, first_head),
        out_shape=[jax.ShapeDtypeStruct((heads, n_type * EXP_CAP, tile), jnp.bfloat16)] * n_query,
        in_specs=[VMEM] * (2 + 2 * n_query),
        out_specs=[VMEM] * n_query,
        scratch_shapes=weigh_scratch(n_type, 1, n_query, tile),
        compiler_params=params(8),
        cost_estimate=cost(0, 16 * tile * tile * heads),
    )(*held([info, key, *queries, *states]))


def finish_kernel(n_type, n_part, info_ref, *refs):
    own_refs, back_refs = refs[:n_part], refs[n_part : 2 * n_part]
    value_refs = refs[2 * n_part : 2 * n_part + n_type]
    out_ref, attended_ref, value_ref = refs[2 * n_part + n_type :]
    me = lax.axis_index("type")
    ends = (me == 0) | (me == n_type - 1)
    tile = out_ref.shape[0]
    width = out_ref.shape[1]
    for s in range(n_type):
        at = pl.multiple_of(jnp.bitwise_xor(me, s) * EXP_CAP, EXP_CAP)
        value_ref[pl.ds(at, EXP_CAP), :] = value_refs[s][...]
    row = lax.broadcasted_iota(jnp.int32, (n_type * EXP_CAP, tile), 0)
    select = (row == info_ref[0:1, :].astype(jnp.int32)).astype(jnp.bfloat16)
    chunk, count = columns(width)
    contract = (((0,), (0,)), ((), ()))
    for c in range(count):
        span = pl.ds(c * chunk, chunk)
        out_ref[:, span] = lax.dot_general(
            select, value_ref[:, span], contract, preferred_element_type=jnp.float32
        ).astype(jnp.bfloat16)
    at = 0
    for part in range(n_part):
        for h in range(own_refs[part].shape[0]):
            span = pl.ds(at * HEAD, HEAD)
            weights = own_refs[part][h]
            if back_refs:
                weights = jnp.where(ends, back_refs[part][h], weights)
            attended_ref[:, span] = lax.dot_general(
                weights, value_ref[:, span], contract, preferred_element_type=jnp.float32
            ).astype(jnp.bfloat16)
            at += 1


def finish(n_type, info, own, back, values, tile):
    width = values[0].shape[1]
    n_part = len(own)
    return pl.pallas_call(
        functools.partial(finish_kernel, n_type, n_part),
        out_shape=[jax.ShapeDtypeStruct((tile, width), jnp.bfloat16)] * 2,
        in_specs=[VMEM] * (1 + 2 * n_part + n_type),
        out_specs=[VMEM] * 2,
        scratch_shapes=[pltpu.VMEM((n_type * EXP_CAP, width), jnp.bfloat16)],
        compiler_params=params(8),
        cost_estimate=cost(0, 0),
    )(*held([info, *own, *back, *values]))


def swap(x, axis, size, s):
    return lax.ppermute(x, axis, [(i, i ^ s) for i in range(size)])


def as_one_step(fn, *operands):
    shapes = jax.eval_shape(fn, *operands)
    blank = lambda *_: jax.tree.map(lambda x: jnp.zeros(x.shape, x.dtype), shapes)
    return lax.cond(lax.axis_index("type") >= 0, fn, blank, *operands)


def on_device(n_dp, n_type, tokens, token_types, tile_mask, queries, keys, gate_weight, up_weight, down_weight):
    tile, width = tokens.shape
    heads = width // HEAD
    tie = lax.optimization_barrier
    n_same = n_dp // 2
    outgoing = route(n_type, token_types.reshape(1, tile), tile_mask.reshape(1, n_type), tokens)
    incoming = [outgoing[0]] + [swap(outgoing[s], "type", n_type, s) for s in range(1, n_type)]

    def experts(incoming, *weights):
        packed, info = pack(n_type, incoming)
        weights = fetch(weights)
        rows = [packed]
        for p in range(1, n_same):
            low = p & -p
            rows.append(swap(rows[p - low], "dp", n_dp, 2 * low))
        rows, weights = tie((rows, weights))
        same_core = jnp.concatenate(rows, axis=0)
        return info, *ffn(same_core, swap(same_core, "dp", n_dp, 1), *weights)

    def gather_sum(own_rows, away_rows, *beside):
        chip_rows = own_rows + swap(away_rows, "dp", n_dp, 1).astype(jnp.float32)
        chip_rows = chip_rows.astype(jnp.bfloat16)
        pieces = [chip_rows[p * EXP_CAP : (p + 1) * EXP_CAP] for p in range(n_same)]
        pieces = [pieces[0]] + [swap(pieces[p], "dp", n_dp, 2 * p) for p in range(1, n_same)]
        state = None
        if beside:
            info, queries, *tiles = beside
            state = weigh_begin(n_type, info, queries, 0, tiles, [0, 1, 3])
            pieces, state = tie((pieces, state))
        total = pieces[0].astype(jnp.float32)
        for piece in pieces[1:]:
            total = total + piece.astype(jnp.float32)
        return total.astype(jnp.bfloat16), state

    weights = (gate_weight[0], up_weight[0], down_weight[0])
    if n_type == 4:
        to_middle = [(0, 1), (3, 2)]
        across = [(1, 2), (2, 1)]
        to_end = [(1, 0), (2, 3)]
        incoming, keys, queries = tie((incoming, keys, queries))
        near = lax.ppermute(keys, "type", to_middle)
        other = lax.ppermute(keys, "type", across)
        guest = lax.ppermute(queries, "type", to_middle)
        info, own_rows, away_rows = as_one_step(experts, incoming, *weights)
        own_rows, near, other = tie((own_rows, near, other))
        far = lax.ppermute(near, "type", across)
        expert_rows, state = as_one_step(
            gather_sum, own_rows, away_rows, info, queries, keys, near, other
        )
        values = [expert_rows] + [swap(expert_rows, "type", n_type, s) for s in range(1, n_type)]
        expert_rows, guest, far = tie((expert_rows, guest, far))
        guest_state = weigh_begin(n_type, info, guest, 1, [keys, near, other], [0, 1, 3])
        own_weights, back_weights = [], []
        ends = [0, heads // 2, heads - heads // 8, heads]
        for first, last in zip(ends[:-1], ends[1:]):
            own, theirs = weigh_end(
                n_type, info, far, 2, [queries, guest], [state, guest_state], first, last - first
            )
            own_weights.append(own)
            back_weights.append(lax.ppermute(theirs, "type", to_end))
    else:
        info, own_rows, away_rows = experts(incoming, *weights)
        expert_rows, _ = gather_sum(own_rows, away_rows)
        values = [expert_rows] + [swap(expert_rows, "type", n_type, s) for s in range(1, n_type)]
        tiles = [keys] + [swap(keys, "type", n_type, s) for s in range(1, n_type)]
        state = weigh_begin(n_type, info, queries, 0, tiles[:-1], list(range(n_type - 1)))
        own_weights = list(
            weigh_end(n_type, info, tiles[-1], n_type - 1, [queries], [state], 0, heads)
        )
        back_weights = own_weights
    expert_out, attended = finish(n_type, info, own_weights, back_weights, values, tile)
    return (expert_out, attended)


def solution(mesh):
    return jax.shard_map(
        functools.partial(on_device, mesh.shape["dp"], mesh.shape["type"]),
        mesh=mesh,
        in_specs=(
            P(("dp", "type"), None),
            P(("dp", "type"), None),
            P("dp", "type", None),
            P(("dp", "type"), None),
            P(("dp", "type"), None),
            P("type", None, "dp"),
            P("type", None, "dp"),
            P("type", "dp", None),
        ),
        out_specs=(P(("dp", "type"), None), P(("dp", "type"), None)),
        check_vma=False,
    )
```

```python
import functools
import math

import jax
import jax.numpy as jnp
from jax import lax
from jax.experimental import pallas as pl
from jax.experimental.pallas import tpu as pltpu
from jax.sharding import PartitionSpec as P

HEAD = 128
EXP_CAP = 16
LANES = 128
MASKED = -1e30
MIB = 1024 * 1024
VMEM = pl.BlockSpec(memory_space=pltpu.VMEM)


def params(mib, **more):
    return pltpu.CompilerParams(vmem_limit_bytes=mib * MIB, **more)


def held(arrays):
    return [pltpu.with_memory_space_constraint(x, pltpu.VMEM) for x in arrays]


def cost(flops, bytes_accessed, transcendentals=0):
    return pl.CostEstimate(
        flops=int(flops), bytes_accessed=int(bytes_accessed), transcendentals=int(transcendentals)
    )


def strict_upper(size):
    earlier = lax.broadcasted_iota(jnp.int32, (size, size), 0)
    later = lax.broadcasted_iota(jnp.int32, (size, size), 1)
    return (earlier < later).astype(jnp.bfloat16)


def columns(width):
    for chunk in (1024, 512, 256, 128):
        if width % chunk == 0:
            return chunk, width // chunk
    raise ValueError(width)


def route_kernel(n_type, types_ref, mask_ref, tokens_ref, *refs):
    out_refs, select_ref = refs[:n_type], refs[n_type]
    me = lax.axis_index("type")
    step = pl.program_id(0)
    rows, chunk = tokens_ref.shape
    width = out_refs[0].shape[1] - LANES

    @pl.when(step == 0)
    def _():
        types = types_ref[...]
        hot = lax.broadcasted_iota(jnp.int32, (EXP_CAP, rows), 0) == types
        before = jnp.dot(
            hot.astype(jnp.bfloat16), strict_upper(rows), preferred_element_type=jnp.float32
        )
        rank = jnp.sum(jnp.where(hot, before, 0.0), axis=0, keepdims=True).astype(jnp.int32)
        place = jnp.where(rank < EXP_CAP, jnp.bitwise_xor(types, me) * EXP_CAP + rank, -1)
        select_ref[...] = (
            lax.broadcasted_iota(jnp.int32, (n_type * EXP_CAP, rows), 0) == place
        ).astype(jnp.bfloat16)
        lane = lax.broadcasted_iota(jnp.int32, (EXP_CAP, LANES), 1)
        row = lax.broadcasted_iota(jnp.int32, (EXP_CAP, LANES), 0)
        mask_row = jnp.zeros((EXP_CAP, LANES), jnp.int32)
        for j in range(n_type):
            mask_row = jnp.where(lane == j, mask_ref[0, j], mask_row)
        extra = jnp.where(row == 0, types, jnp.where(row == 1, mask_row, 0))
        extra = extra.astype(jnp.float32).astype(jnp.bfloat16)
        for s in range(n_type):
            out_refs[s][:, pl.ds(width, LANES)] = extra

    moved = jnp.dot(select_ref[...], tokens_ref[...], preferred_element_type=jnp.float32).astype(
        jnp.bfloat16
    )
    span = pl.ds(pl.multiple_of(step * chunk, chunk), chunk)
    for s in range(n_type):
        out_refs[s][:, span] = moved[s * EXP_CAP : (s + 1) * EXP_CAP]


def route(n_type, types, mask_row, tokens):
    rows, width = tokens.shape
    wide = width + LANES
    chunk, count = columns(width)
    return pl.pallas_call(
        functools.partial(route_kernel, n_type),
        grid=(count,),
        out_shape=[jax.ShapeDtypeStruct((EXP_CAP, wide), jnp.bfloat16)] * n_type,
        in_specs=[
            VMEM,
            pl.BlockSpec(memory_space=pltpu.SMEM),
            pl.BlockSpec((rows, chunk), lambda i: (0, i)),
        ],
        out_specs=[VMEM] * n_type,
        scratch_shapes=[pltpu.VMEM((n_type * EXP_CAP, rows), jnp.bfloat16)],
        compiler_params=params(8, dimension_semantics=("arbitrary",)),
        cost_estimate=cost(0, 0),
    )(*[pltpu.with_memory_space_constraint(x, pltpu.HBM) for x in (types, mask_row, tokens)])


def fetch_kernel(count, *refs):
    sems = refs[2 * count]
    copies = [pltpu.make_async_copy(refs[i], refs[count + i], sems.at[i]) for i in range(count)]
    for copy in copies:
        copy.start()
    for copy in copies:
        copy.wait()


def fetch(arrays):
    count = len(arrays)
    return pl.pallas_call(
        functools.partial(fetch_kernel, count),
        out_shape=[pltpu.VMEM(x.shape, x.dtype) for x in arrays],
        in_specs=[pl.BlockSpec(memory_space=pl.ANY)] * count,
        out_specs=[VMEM] * count,
        scratch_shapes=[pltpu.SemaphoreType.DMA((count,))],
        compiler_params=params(1),
        cost_estimate=cost(0, 2 * sum(x.size * 2 for x in arrays)),
    )(*[pltpu.with_memory_space_constraint(x, pltpu.HBM) for x in arrays])


def pack_kernel(n_type, *refs):
    in_refs, packed_ref, info_ref = refs[:n_type], refs[n_type], refs[n_type + 1]
    me = lax.axis_index("type")
    width = packed_ref.shape[1]
    tail = pl.ds(width, LANES)
    type_rows = 2 * 8
    row = lax.broadcasted_iota(jnp.int32, (type_rows, LANES), 0)
    upper = strict_upper(LANES)
    extras = [ref[:, tail].astype(jnp.float32) for ref in in_refs]
    types = [e[0:1] for e in extras]
    hots = [row == t.astype(jnp.int32) for t in types]
    befores = [
        jnp.dot(h.astype(jnp.bfloat16), upper, preferred_element_type=jnp.float32) for h in hots
    ]
    counts = [jnp.sum(h.astype(jnp.float32), axis=1, keepdims=True) for h in hots]
    lane16 = lax.broadcasted_iota(jnp.int32, (EXP_CAP, n_type * EXP_CAP), 1)
    slot16 = lax.broadcasted_iota(jnp.int32, (EXP_CAP, n_type * EXP_CAP), 0)
    compact = jnp.zeros((EXP_CAP, n_type * EXP_CAP), jnp.bool_)
    mine = lax.broadcasted_iota(jnp.int32, (type_rows, 1), 0) == me
    info_rows = []
    for s in range(n_type):
        ahead = jnp.zeros((type_rows, 1), jnp.float32)
        for other in range(n_type):
            if other != s:
                first = jnp.bitwise_xor(me, other) < jnp.bitwise_xor(me, s)
                ahead = ahead + jnp.where(first, counts[other], 0.0)
        rank = jnp.sum(jnp.where(hots[s], befores[s] + ahead, 0.0), axis=0, keepdims=True)
        info_rows.append(jnp.where(rank < EXP_CAP, types[s] * EXP_CAP + rank, -1.0))
        offset = jnp.sum(jnp.where(mine, ahead, 0.0)).astype(jnp.int32)
        amount = jnp.sum(jnp.where(mine, counts[s], 0.0)).astype(jnp.int32)
        local = lane16 - s * EXP_CAP
        compact = compact | (
            (local >= 0) & (local < EXP_CAP) & (local < amount) & (local + offset == slot16)
        )
    lane = lax.broadcasted_iota(jnp.int32, (1, LANES), 1)
    for q in range(2):
        for s in range(n_type):
            kept = jnp.sum(
                jnp.where(lane == jnp.bitwise_xor(me, s), extras[q][1:2], 0.0),
                axis=1,
                keepdims=True,
            )
            info_rows.append(jnp.broadcast_to(jnp.where(kept == 1.0, 0.0, MASKED), (1, LANES)))
    for at, info_row in enumerate(info_rows):
        info_ref[at : at + 1, :] = info_row
    compact = compact.astype(jnp.bfloat16)
    chunk, count = columns(width)
    for c in range(count):
        span = pl.ds(c * chunk, chunk)
        rows = jnp.concatenate([ref[:, span] for ref in in_refs], axis=0)
        packed_ref[:, span] = jnp.dot(compact, rows, preferred_element_type=jnp.float32).astype(
            jnp.bfloat16
        )


def pack(n_type, incoming):
    width = incoming[0].shape[1] - LANES
    return pl.pallas_call(
        functools.partial(pack_kernel, n_type),
        out_shape=[
            jax.ShapeDtypeStruct((EXP_CAP, width), jnp.bfloat16),
            jax.ShapeDtypeStruct((3 * n_type, LANES), jnp.float32),
        ],
        in_specs=[VMEM] * n_type,
        out_specs=[VMEM, VMEM],
        compiler_params=params(8),
        cost_estimate=cost(0, 0),
    )(*held(incoming))


def ffn_kernel(near_ref, far_ref, gate_ref, up_ref, down_ref, own_ref, away_ref, x_ref, hidden_ref):
    half = near_ref.shape[0]
    x_ref[:half] = near_ref[...]
    x_ref[half:] = far_ref[...]
    hidden = gate_ref.shape[1]
    for at in range(0, hidden, 256):
        span = pl.ds(at, min(256, hidden - at))
        gate = jnp.dot(x_ref[...], gate_ref[:, span], preferred_element_type=jnp.float32)
        up = jnp.dot(x_ref[...], up_ref[:, span], preferred_element_type=jnp.float32)
        hidden_ref[:, span] = (gate / (1.0 + jnp.exp(-gate)) * up).astype(jnp.bfloat16)
    for at in range(0, down_ref.shape[1], 512):
        span = pl.ds(at, 512)
        out = jnp.dot(hidden_ref[...], down_ref[:, span], preferred_element_type=jnp.float32)
        own_ref[:, span] = out[:half]
        away_ref[:, span] = out[half:].astype(jnp.bfloat16)


def ffn(near, far, gate, up, down):
    half, width = near.shape
    rows = 2 * half
    hidden = gate.shape[1]
    return pl.pallas_call(
        ffn_kernel,
        out_shape=[
            jax.ShapeDtypeStruct((half, width), jnp.float32),
            jax.ShapeDtypeStruct((half, width), jnp.bfloat16),
        ],
        in_specs=[VMEM] * 5,
        out_specs=[VMEM] * 2,
        scratch_shapes=[
            pltpu.VMEM((rows, width), jnp.bfloat16),
            pltpu.VMEM((rows, hidden), jnp.bfloat16),
        ],
        compiler_params=params(16),
        cost_estimate=cost(0, 0),
    )(*held([near, far, gate, up, down]))


FACTOR = math.log2(math.e) / math.sqrt(HEAD)


def slots_of(slots, tile, s, info_ref):
    row = lax.broadcasted_iota(jnp.int32, (slots, tile), 0)
    return row == info_ref[s : s + 1, :].astype(jnp.int32)


def mask_row(n_type, q, s, info_ref):
    line = (1 + q) * n_type + s
    return info_ref[line : line + 1, :]


def product(rows, queries):
    return lax.dot_general(
        rows, queries, (((1,), (1,)), ((), ())), preferred_element_type=jnp.float32
    )


def pair_of(query):
    lane = lax.broadcasted_iota(jnp.int32, query.shape, 1)
    zero = jnp.zeros_like(query)
    return jnp.concatenate(
        [jnp.where(lane < HEAD, query, zero), jnp.where(lane >= HEAD, query, zero)], axis=0
    )


def pair_scores(n_type, q, tile_ids, info_ref, key_refs, query_ref, span):
    tile = query_ref.shape[0]
    scores = product(
        jnp.concatenate([ref[:, span] for ref in key_refs], axis=0), pair_of(query_ref[:, span])
    )
    scores = [scores[i * tile : (i + 1) * tile] for i in range(len(tile_ids))]
    masks = [mask_row(n_type, q, s, info_ref) for s in tile_ids]
    return [x + jnp.concatenate([m, m], axis=1) for x, m in zip(scores, masks)]


def top_of(scores):
    return functools.reduce(jnp.maximum, [jnp.max(x, axis=0, keepdims=True) for x in scores])


def total_of(scores, top):
    return sum(jnp.sum(jnp.exp2((x - top) * FACTOR), axis=0, keepdims=True) for x in scores)


def weigh_begin_kernel(n_type, tile_ids, info_ref, query_ref, *refs):
    key_refs = refs[: len(tile_ids)]
    state_ref, kept_ref = refs[len(tile_ids) :]
    slots, width = kept_ref.shape
    tile = query_ref.shape[0]
    select = [slots_of(slots, tile, s, info_ref).astype(jnp.bfloat16) for s in tile_ids]
    kept_ref[...] = jnp.dot(
        jnp.concatenate(select, axis=1),
        jnp.concatenate([ref[...] for ref in key_refs], axis=0),
        preferred_element_type=jnp.float32,
    ).astype(jnp.bfloat16)
    for at in range(0, width, 2 * HEAD):
        span = pl.ds(at, 2 * HEAD)
        scores = pair_scores(n_type, 0, tile_ids, info_ref, key_refs, query_ref, span)
        top = top_of(scores)
        total = total_of(scores, top)
        for i in range(2):
            mine = slice(i * tile, (i + 1) * tile)
            head = at // HEAD + i
            state_ref[head, :8] = jnp.broadcast_to(total[:, mine], (8, tile))
            state_ref[head, 8:] = jnp.broadcast_to(top[:, mine], (8, tile))


PER_STEP = 4


def weigh_begin(n_type, info, query, keys, tile_ids):
    tile, width = query.shape
    heads = width // HEAD
    slots = n_type * EXP_CAP
    block = pl.BlockSpec((tile, PER_STEP * HEAD), lambda i: (0, i))
    return pl.pallas_call(
        functools.partial(weigh_begin_kernel, n_type, tile_ids),
        grid=(heads // PER_STEP,),
        out_shape=[
            jax.ShapeDtypeStruct((heads, 2 * 8, tile), jnp.float32),
            jax.ShapeDtypeStruct((slots, width), jnp.bfloat16),
        ],
        in_specs=[VMEM] + [block] * (1 + len(keys)),
        out_specs=[
            pl.BlockSpec((PER_STEP, 2 * 8, tile), lambda i: (i, 0, 0)),
            pl.BlockSpec((slots, PER_STEP * HEAD), lambda i: (0, i)),
        ],
        compiler_params=params(16, dimension_semantics=("arbitrary",)),
        cost_estimate=cost(0, 0),
    )(info, query, *keys)


def weigh_end_kernel(n_type, n_query, tile_ids, info_ref, kept_ref, state_ref, last_ref, *refs):
    query_refs, refs = refs[:n_query], refs[n_query:]
    n_key = len(refs) - n_query - 1
    key_refs, refs = refs[:n_key], refs[n_key:]
    out_refs, bias_ref = refs[:n_query], refs[n_query]
    slots, width = kept_ref.shape
    tile = last_ref.shape[0]

    @pl.when(pl.program_id(0) == 0)
    def _():
        bias = [jnp.full((slots, tile), MASKED, jnp.float32) for _ in range(n_query)]
        for s in tile_ids:
            chosen = slots_of(slots, tile, s, info_ref).astype(jnp.float32)
            filled = jnp.max(chosen, axis=1, keepdims=True)
            for q in range(n_query):
                bias[q] = jnp.where(filled > 0.0, mask_row(n_type, q, s, info_ref), bias[q])
        for q in range(n_query):
            bias_ref[:, q * tile : (q + 1) * tile] = bias[q]

    select = slots_of(slots, tile, tile_ids[-1], info_ref).astype(jnp.bfloat16)
    found = jnp.dot(select, last_ref[...], preferred_element_type=jnp.float32)
    kept = (kept_ref[...].astype(jnp.float32) + found).astype(jnp.bfloat16)
    last_mask = jnp.concatenate(
        [mask_row(n_type, q, tile_ids[-1], info_ref) for q in range(n_query)], axis=1
    )
    for at in range(0, width, 2 * HEAD):
        if n_query > 1:
            rest = pair_scores(
                n_type, 1, tile_ids[:-1], info_ref, key_refs, query_refs[1], pl.ds(at, 2 * HEAD)
            )
            rest_top = top_of(rest)
        for i in range(2):
            mine = slice(i * tile, (i + 1) * tile)
            head = at // HEAD + i
            span = slice(head * HEAD, (head + 1) * HEAD)
            scores = product(
                jnp.concatenate([last_ref[:, span], kept[:, span]], axis=0),
                jnp.concatenate([ref[:, span] for ref in query_refs], axis=0),
            )
            last = scores[:tile] + last_mask
            state_top = state_ref[head, 8:9]
            tops = [state_top] + ([rest_top[:, mine]] if n_query > 1 else [])
            top = jnp.maximum(jnp.concatenate(tops, axis=1), jnp.max(last, axis=0, keepdims=True))
            own_top = top[:, :tile]
            before = [state_ref[head, 0:1] * jnp.exp2((state_top - own_top) * FACTOR)]
            if n_query > 1:
                before.append(total_of([x[:, mine] for x in rest], top[:, tile:]))
            total = total_of([last], top) + jnp.concatenate(before, axis=1)
            weights = jnp.exp2((scores[tile:] + bias_ref[...] - top) * FACTOR) * (1.0 / total)
            for q in range(n_query):
                out_refs[q][head] = weights[:, q * tile : (q + 1) * tile].astype(jnp.bfloat16)


def weigh_end(n_type, info, begun, last_key, queries, keys, tile_ids, first_head, heads):
    state, kept = begun
    tile = last_key.shape[0]
    n_query = len(queries)
    slots = n_type * EXP_CAP
    first = first_head // PER_STEP
    block = pl.BlockSpec((tile, PER_STEP * HEAD), lambda i: (0, i + first))
    out_block = pl.BlockSpec((PER_STEP, slots, tile), lambda i: (i, 0, 0))
    return pl.pallas_call(
        functools.partial(weigh_end_kernel, n_type, n_query, tile_ids),
        grid=(heads // PER_STEP,),
        out_shape=[jax.ShapeDtypeStruct((heads, slots, tile), jnp.bfloat16)] * n_query,
        in_specs=[
            VMEM,
            pl.BlockSpec((slots, PER_STEP * HEAD), lambda i: (0, i + first)),
            pl.BlockSpec((PER_STEP, 2 * 8, tile), lambda i: (i + first, 0, 0)),
        ]
        + [block] * (1 + n_query + len(keys)),
        out_specs=[out_block] * n_query,
        scratch_shapes=[pltpu.VMEM((slots, n_query * tile), jnp.float32)],
        compiler_params=params(16, dimension_semantics=("arbitrary",)),
        cost_estimate=cost(0, 16 * tile * tile * heads),
    )(info, kept, state, last_key, *queries, *keys)


def finish_kernel(n_type, n_part, info_ref, *refs):
    own_refs, back_refs = refs[:n_part], refs[n_part : 2 * n_part]
    values_ref, out_ref, attended_ref, value_ref = refs[2 * n_part :]
    me = lax.axis_index("type")
    ends = (me == 0) | (me == n_type - 1)
    tile = out_ref.shape[0]
    width = out_ref.shape[1]
    for s in range(n_type):
        at = pl.multiple_of(jnp.bitwise_xor(me, s) * EXP_CAP, EXP_CAP)
        value_ref[pl.ds(at, EXP_CAP), :] = values_ref[s * EXP_CAP : (s + 1) * EXP_CAP]
    row = lax.broadcasted_iota(jnp.int32, (n_type * EXP_CAP, tile), 0)
    select = (row == info_ref[0:1, :].astype(jnp.int32)).astype(jnp.bfloat16)
    chunk, count = columns(width)
    contract = (((0,), (0,)), ((), ()))
    for c in range(count):
        span = pl.ds(c * chunk, chunk)
        out_ref[:, span] = lax.dot_general(
            select, value_ref[:, span], contract, preferred_element_type=jnp.float32
        ).astype(jnp.bfloat16)
    at = 0
    for part in range(n_part):
        for h in range(own_refs[part].shape[0]):
            span = pl.ds(at * HEAD, HEAD)
            weights = own_refs[part][h]
            if back_refs:
                weights = jnp.where(ends, back_refs[part][h], weights)
            attended_ref[:, span] = lax.dot_general(
                weights, value_ref[:, span], contract, preferred_element_type=jnp.float32
            ).astype(jnp.bfloat16)
            at += 1


def finish(n_type, info, own, back, values, tile):
    width = values.shape[1]
    n_part = len(own)
    return pl.pallas_call(
        functools.partial(finish_kernel, n_type, n_part),
        out_shape=[jax.ShapeDtypeStruct((tile, width), jnp.bfloat16)] * 2,
        in_specs=[VMEM] * (2 + 2 * n_part),
        out_specs=[VMEM] * 2,
        scratch_shapes=[pltpu.VMEM((n_type * EXP_CAP, width), jnp.bfloat16)],
        compiler_params=params(8),
        cost_estimate=cost(0, 0),
    )(*held([info, *own, *back, values]))


def swap(x, axis, size, s):
    return lax.ppermute(x, axis, [(i, i ^ s) for i in range(size)])


def as_one_step(fn, *operands):
    shapes = jax.eval_shape(fn, *operands)
    blank = lambda *_: jax.tree.map(lambda x: jnp.zeros(x.shape, x.dtype), shapes)
    return lax.cond(lax.axis_index("type") >= 0, fn, blank, *operands)


def on_device(n_dp, n_type, tokens, token_types, tile_mask, queries, keys, gate_weight, up_weight, down_weight):
    tile, width = tokens.shape
    heads = width // HEAD
    tie = lax.optimization_barrier
    n_same = n_dp // 2
    outgoing = route(n_type, token_types.reshape(1, tile), tile_mask.reshape(1, n_type), tokens)
    incoming = [outgoing[0]] + [swap(outgoing[s], "type", n_type, s) for s in range(1, n_type)]

    def experts(incoming, *weights):
        packed, info = pack(n_type, incoming)
        weights = fetch(weights)
        rows = [packed]
        for p in range(1, n_same):
            low = p & -p
            rows.append(swap(rows[p - low], "dp", n_dp, 2 * low))
        rows, weights = tie((rows, weights))
        same_core = jnp.concatenate(rows, axis=0)
        return info, *ffn(same_core, swap(same_core, "dp", n_dp, 1), *weights)

    def gather_sum(own_rows, away_rows, *beside):
        chip_rows = own_rows + swap(away_rows, "dp", n_dp, 1).astype(jnp.float32)
        chip_rows = chip_rows.astype(jnp.bfloat16)
        pieces = [chip_rows[p * EXP_CAP : (p + 1) * EXP_CAP] for p in range(n_same)]
        pieces = [pieces[0]] + [swap(pieces[p], "dp", n_dp, 2 * p) for p in range(1, n_same)]
        begun = None
        if beside:
            begun = weigh_begin(n_type, *beside, [0, 1, 3])
            pieces, begun = tie((pieces, begun))
        total = pieces[0].astype(jnp.float32)
        for piece in pieces[1:]:
            total = total + piece.astype(jnp.float32)
        expert_rows = total.astype(jnp.bfloat16)
        return jnp.concatenate([expert_rows, swap(expert_rows, "type", n_type, 1)], axis=0), begun

    def spread(rows):
        step = 2
        while step < n_type:
            rows = jnp.concatenate([rows, swap(rows, "type", n_type, step)], axis=0)
            step *= 2
        return rows

    weights = (gate_weight[0], up_weight[0], down_weight[0])
    if n_type == 4:
        to_middle = [(0, 1), (3, 2)]
        across = [(1, 2), (2, 1)]
        to_end = [(1, 0), (2, 3)]
        incoming, keys, queries = tie((incoming, keys, queries))
        near = lax.ppermute(keys, "type", to_middle)
        other = lax.ppermute(keys, "type", across)
        guest = lax.ppermute(queries, "type", to_middle)
        info, own_rows, away_rows = as_one_step(experts, incoming, *weights)
        own_rows, near = tie((own_rows, near))
        far = lax.ppermute(near, "type", across)
        expert_rows, begun = as_one_step(
            gather_sum, own_rows, away_rows, info, queries, [keys, near, other]
        )
        values = spread(expert_rows)
        expert_rows, begun, guest, far = tie((expert_rows, begun, guest, far))
        own_weights, back_weights = [], []
        ends = [0, heads // 2 + PER_STEP, heads]
        for first, last in zip(ends[:-1], ends[1:]):
            own, theirs = weigh_end(
                n_type,
                info,
                begun,
                far,
                [queries, guest],
                [keys, near, other],
                [0, 1, 3, 2],
                first,
                last - first,
            )
            own_weights.append(own)
            back_weights.append(lax.ppermute(theirs, "type", to_end))
    else:
        info, own_rows, away_rows = experts(incoming, *weights)
        expert_rows, _ = gather_sum(own_rows, away_rows)
        values = spread(expert_rows)
        tiles = [keys] + [swap(keys, "type", n_type, s) for s in range(1, n_type)]
        ids = list(range(n_type))
        begun = weigh_begin(n_type, info, queries, tiles[:-1], ids[:-1])
        own_weights = list(
            weigh_end(n_type, info, begun, tiles[-1], [queries], [], ids, 0, heads)
        )
        back_weights = own_weights
    expert_out, attended = finish(n_type, info, own_weights, back_weights, values, tile)
    return (expert_out, attended)


def solution(mesh):
    return jax.shard_map(
        functools.partial(on_device, mesh.shape["dp"], mesh.shape["type"]),
        mesh=mesh,
        in_specs=(
            P(("dp", "type"), None),
            P(("dp", "type"), None),
            P("dp", "type", None),
            P(("dp", "type"), None),
            P(("dp", "type"), None),
            P("type", None, "dp"),
            P("type", None, "dp"),
            P("type", "dp", None),
        ),
        out_specs=(P(("dp", "type"), None), P(("dp", "type"), None)),
        check_vma=False,
    )
```

```python
import functools
import math

import jax
import jax.numpy as jnp
from jax import lax
from jax.experimental import pallas as pl
from jax.experimental.pallas import tpu as pltpu
from jax.sharding import PartitionSpec as P

HEAD = 128
EXP_CAP = 16
LANES = 128
MASKED = -1e30
MIB = 1024 * 1024
VMEM = pl.BlockSpec(memory_space=pltpu.VMEM)


def params(mib, **more):
    return pltpu.CompilerParams(vmem_limit_bytes=mib * MIB, **more)


def held(arrays):
    return [pltpu.with_memory_space_constraint(x, pltpu.VMEM) for x in arrays]


def cost(flops, bytes_accessed, transcendentals=0):
    return pl.CostEstimate(
        flops=int(flops), bytes_accessed=int(bytes_accessed), transcendentals=int(transcendentals)
    )


def strict_upper(size):
    earlier = lax.broadcasted_iota(jnp.int32, (size, size), 0)
    later = lax.broadcasted_iota(jnp.int32, (size, size), 1)
    return (earlier < later).astype(jnp.bfloat16)


def columns(width):
    for chunk in (1024, 512, 256, 128):
        if width % chunk == 0:
            return chunk, width // chunk
    raise ValueError(width)


def route_kernel(n_type, types_ref, mask_ref, tokens_ref, *refs):
    out_refs, select_ref = refs[:n_type], refs[n_type]
    me = lax.axis_index("type")
    step = pl.program_id(0)
    rows, chunk = tokens_ref.shape
    width = out_refs[0].shape[1] - LANES

    @pl.when(step == 0)
    def _():
        types = types_ref[...]
        hot = lax.broadcasted_iota(jnp.int32, (EXP_CAP, rows), 0) == types
        before = jnp.dot(
            hot.astype(jnp.bfloat16), strict_upper(rows), preferred_element_type=jnp.float32
        )
        rank = jnp.sum(jnp.where(hot, before, 0.0), axis=0, keepdims=True).astype(jnp.int32)
        place = jnp.where(rank < EXP_CAP, jnp.bitwise_xor(types, me) * EXP_CAP + rank, -1)
        select_ref[...] = (
            lax.broadcasted_iota(jnp.int32, (n_type * EXP_CAP, rows), 0) == place
        ).astype(jnp.bfloat16)
        lane = lax.broadcasted_iota(jnp.int32, (EXP_CAP, LANES), 1)
        row = lax.broadcasted_iota(jnp.int32, (EXP_CAP, LANES), 0)
        mask_row = jnp.zeros((EXP_CAP, LANES), jnp.int32)
        for j in range(n_type):
            mask_row = jnp.where(lane == j, mask_ref[0, j], mask_row)
        extra = jnp.where(row == 0, types, jnp.where(row == 1, mask_row, 0))
        extra = extra.astype(jnp.float32).astype(jnp.bfloat16)
        for s in range(n_type):
            out_refs[s][:, pl.ds(width, LANES)] = extra

    moved = jnp.dot(select_ref[...], tokens_ref[...], preferred_element_type=jnp.float32).astype(
        jnp.bfloat16
    )
    span = pl.ds(pl.multiple_of(step * chunk, chunk), chunk)
    for s in range(n_type):
        out_refs[s][:, span] = moved[s * EXP_CAP : (s + 1) * EXP_CAP]


def route(n_type, types, mask_row, tokens):
    rows, width = tokens.shape
    wide = width + LANES
    chunk, count = columns(width)
    return pl.pallas_call(
        functools.partial(route_kernel, n_type),
        grid=(count,),
        out_shape=[jax.ShapeDtypeStruct((EXP_CAP, wide), jnp.bfloat16)] * n_type,
        in_specs=[
            VMEM,
            pl.BlockSpec(memory_space=pltpu.SMEM),
            pl.BlockSpec((rows, chunk), lambda i: (0, i)),
        ],
        out_specs=[VMEM] * n_type,
        scratch_shapes=[pltpu.VMEM((n_type * EXP_CAP, rows), jnp.bfloat16)],
        compiler_params=params(8, dimension_semantics=("arbitrary",)),
        cost_estimate=cost(0, 0),
    )(*[pltpu.with_memory_space_constraint(x, pltpu.HBM) for x in (types, mask_row, tokens)])


def fetch_kernel(count, *refs):
    sems = refs[2 * count]
    copies = [pltpu.make_async_copy(refs[i], refs[count + i], sems.at[i]) for i in range(count)]
    for copy in copies:
        copy.start()
    for copy in copies:
        copy.wait()


def fetch(arrays):
    count = len(arrays)
    return pl.pallas_call(
        functools.partial(fetch_kernel, count),
        out_shape=[pltpu.VMEM(x.shape, x.dtype) for x in arrays],
        in_specs=[pl.BlockSpec(memory_space=pl.ANY)] * count,
        out_specs=[VMEM] * count,
        scratch_shapes=[pltpu.SemaphoreType.DMA((count,))],
        compiler_params=params(1),
        cost_estimate=cost(0, 2 * sum(x.size * 2 for x in arrays)),
    )(*[pltpu.with_memory_space_constraint(x, pltpu.HBM) for x in arrays])


def pack_kernel(n_type, *refs):
    in_refs, packed_ref, info_ref = refs[:n_type], refs[n_type], refs[n_type + 1]
    me = lax.axis_index("type")
    width = packed_ref.shape[1]
    tail = pl.ds(width, LANES)
    type_rows = 2 * 8
    row = lax.broadcasted_iota(jnp.int32, (type_rows, LANES), 0)
    upper = strict_upper(LANES)
    extras = [ref[:, tail].astype(jnp.float32) for ref in in_refs]
    types = [e[0:1] for e in extras]
    hots = [row == t.astype(jnp.int32) for t in types]
    befores = [
        jnp.dot(h.astype(jnp.bfloat16), upper, preferred_element_type=jnp.float32) for h in hots
    ]
    counts = [jnp.sum(h.astype(jnp.float32), axis=1, keepdims=True) for h in hots]
    lane16 = lax.broadcasted_iota(jnp.int32, (EXP_CAP, n_type * EXP_CAP), 1)
    slot16 = lax.broadcasted_iota(jnp.int32, (EXP_CAP, n_type * EXP_CAP), 0)
    compact = jnp.zeros((EXP_CAP, n_type * EXP_CAP), jnp.bool_)
    mine = lax.broadcasted_iota(jnp.int32, (type_rows, 1), 0) == me
    info_rows = []
    for s in range(n_type):
        ahead = jnp.zeros((type_rows, 1), jnp.float32)
        for other in range(n_type):
            if other != s:
                first = jnp.bitwise_xor(me, other) < jnp.bitwise_xor(me, s)
                ahead = ahead + jnp.where(first, counts[other], 0.0)
        rank = jnp.sum(jnp.where(hots[s], befores[s] + ahead, 0.0), axis=0, keepdims=True)
        info_rows.append(jnp.where(rank < EXP_CAP, types[s] * EXP_CAP + rank, -1.0))
        offset = jnp.sum(jnp.where(mine, ahead, 0.0)).astype(jnp.int32)
        amount = jnp.sum(jnp.where(mine, counts[s], 0.0)).astype(jnp.int32)
        local = lane16 - s * EXP_CAP
        compact = compact | (
            (local >= 0) & (local < EXP_CAP) & (local < amount) & (local + offset == slot16)
        )
    lane = lax.broadcasted_iota(jnp.int32, (1, LANES), 1)
    for q in range(2):
        for s in range(n_type):
            kept = jnp.sum(
                jnp.where(lane == jnp.bitwise_xor(me, s), extras[q][1:2], 0.0),
                axis=1,
                keepdims=True,
            )
            info_rows.append(jnp.broadcast_to(jnp.where(kept == 1.0, 0.0, MASKED), (1, LANES)))
    for at, info_row in enumerate(info_rows):
        info_ref[at : at + 1, :] = info_row
    compact = compact.astype(jnp.bfloat16)
    chunk, count = columns(width)
    for c in range(count):
        span = pl.ds(c * chunk, chunk)
        rows = jnp.concatenate([ref[:, span] for ref in in_refs], axis=0)
        packed_ref[:, span] = jnp.dot(compact, rows, preferred_element_type=jnp.float32).astype(
            jnp.bfloat16
        )


def pack(n_type, incoming):
    width = incoming[0].shape[1] - LANES
    return pl.pallas_call(
        functools.partial(pack_kernel, n_type),
        out_shape=[
            jax.ShapeDtypeStruct((EXP_CAP, width), jnp.bfloat16),
            jax.ShapeDtypeStruct((3 * n_type, LANES), jnp.float32),
        ],
        in_specs=[VMEM] * n_type,
        out_specs=[VMEM, VMEM],
        compiler_params=params(8),
        cost_estimate=cost(0, 0),
    )(*held(incoming))


def ffn_kernel(near_ref, far_ref, gate_ref, up_ref, down_ref, own_ref, away_ref, x_ref, hidden_ref):
    half = near_ref.shape[0]
    x_ref[:half] = near_ref[...]
    x_ref[half:] = far_ref[...]
    hidden = gate_ref.shape[1]
    for at in range(0, hidden, 256):
        span = pl.ds(at, min(256, hidden - at))
        gate = jnp.dot(x_ref[...], gate_ref[:, span], preferred_element_type=jnp.float32)
        up = jnp.dot(x_ref[...], up_ref[:, span], preferred_element_type=jnp.float32)
        hidden_ref[:, span] = (gate / (1.0 + jnp.exp(-gate)) * up).astype(jnp.bfloat16)
    for at in range(0, down_ref.shape[1], 512):
        span = pl.ds(at, 512)
        out = jnp.dot(hidden_ref[...], down_ref[:, span], preferred_element_type=jnp.float32)
        own_ref[:, span] = out[:half]
        away_ref[:, span] = out[half:].astype(jnp.bfloat16)


def ffn(near, far, gate, up, down):
    half, width = near.shape
    rows = 2 * half
    hidden = gate.shape[1]
    return pl.pallas_call(
        ffn_kernel,
        out_shape=[
            jax.ShapeDtypeStruct((half, width), jnp.float32),
            jax.ShapeDtypeStruct((half, width), jnp.bfloat16),
        ],
        in_specs=[VMEM] * 5,
        out_specs=[VMEM] * 2,
        scratch_shapes=[
            pltpu.VMEM((rows, width), jnp.bfloat16),
            pltpu.VMEM((rows, hidden), jnp.bfloat16),
        ],
        compiler_params=params(16),
        cost_estimate=cost(0, 0),
    )(*held([near, far, gate, up, down]))


FACTOR = math.log2(math.e) / math.sqrt(HEAD)


def slots_of(slots, tile, s, info_ref):
    row = lax.broadcasted_iota(jnp.int32, (slots, tile), 0)
    return row == info_ref[s : s + 1, :].astype(jnp.int32)


def mask_row(n_type, q, s, info_ref):
    line = (1 + q) * n_type + s
    return info_ref[line : line + 1, :]


def product(rows, queries):
    return lax.dot_general(
        rows, queries, (((1,), (1,)), ((), ())), preferred_element_type=jnp.float32
    )


def pair_of(query):
    lane = lax.broadcasted_iota(jnp.int32, query.shape, 1)
    zero = jnp.zeros_like(query)
    return jnp.concatenate(
        [jnp.where(lane < HEAD, query, zero), jnp.where(lane >= HEAD, query, zero)], axis=0
    )


def pair_scores(n_type, q, tile_ids, info_ref, key_refs, query_ref, span):
    tile = query_ref.shape[0]
    scores = product(
        jnp.concatenate([ref[:, span] for ref in key_refs], axis=0), pair_of(query_ref[:, span])
    )
    scores = [scores[i * tile : (i + 1) * tile] for i in range(len(tile_ids))]
    masks = [mask_row(n_type, q, s, info_ref) for s in tile_ids]
    return [x + jnp.concatenate([m, m], axis=1) for x, m in zip(scores, masks)]


def top_of(scores):
    return functools.reduce(jnp.maximum, [jnp.max(x, axis=0, keepdims=True) for x in scores])


def total_of(scores, top):
    return sum(jnp.sum(jnp.exp2((x - top) * FACTOR), axis=0, keepdims=True) for x in scores)


def in_middle(body, n_type, *args):
    me = lax.axis_index("type")
    step = pl.program_id(0)
    if n_type != 4:
        body(step, n_type, *args)
    else:

        @pl.when((me > 0) & (me < n_type - 1))
        def _():
            body(step, n_type, *args)


def weigh_begin_body(step, n_type, tile_ids, query_id, info_ref, query_ref, *refs):
    key_refs = refs[: len(tile_ids)]
    state_ref, *kept_refs = refs[len(tile_ids) :]
    tile, width = query_ref.shape
    for kept_ref in kept_refs:
        slots = kept_ref.shape[0]
        select = [slots_of(slots, tile, s, info_ref).astype(jnp.bfloat16) for s in tile_ids]
        kept_ref[...] = jnp.dot(
            jnp.concatenate(select, axis=1),
            jnp.concatenate([ref[...] for ref in key_refs], axis=0),
            preferred_element_type=jnp.float32,
        ).astype(jnp.bfloat16)
    for at in range(0, width, 2 * HEAD):
        span = pl.ds(at, 2 * HEAD)
        scores = pair_scores(n_type, query_id, tile_ids, info_ref, key_refs, query_ref, span)
        top = top_of(scores)
        total = total_of(scores, top)
        for i in range(2):
            mine = slice(i * tile, (i + 1) * tile)
            head = at // HEAD + i
            state_ref[head, :8] = jnp.broadcast_to(total[:, mine], (8, tile))
            state_ref[head, 8:] = jnp.broadcast_to(top[:, mine], (8, tile))


PER_STEP = 8


def weigh_begin(n_type, info, query, query_id, keys, tile_ids):
    tile, width = query.shape
    heads = width // HEAD
    slots = n_type * EXP_CAP
    block = pl.BlockSpec((tile, PER_STEP * HEAD), lambda i: (0, i))
    return pl.pallas_call(
        functools.partial(in_middle, weigh_begin_body, n_type, tile_ids, query_id),
        grid=(heads // PER_STEP,),
        out_shape=[
            jax.ShapeDtypeStruct((heads, 2 * 8, tile), jnp.float32),
            jax.ShapeDtypeStruct((slots, width), jnp.bfloat16),
        ][: 2 - query_id],
        in_specs=[VMEM] + [block] * (1 + len(keys)),
        out_specs=[
            pl.BlockSpec((PER_STEP, 2 * 8, tile), lambda i: (i, 0, 0)),
            pl.BlockSpec((slots, PER_STEP * HEAD), lambda i: (0, i)),
        ][: 2 - query_id],
        compiler_params=params(16, dimension_semantics=("arbitrary",)),
        cost_estimate=cost(0, 16 * tile * tile * heads),
    )(info, query, *keys)


def weigh_end_body(step, n_type, tile_ids, info_ref, kept_ref, last_ref, *refs):
    n_query = (len(refs) - 1) // 3
    query_refs, state_refs = refs[:n_query], refs[n_query : 2 * n_query]
    out_refs, bias_ref = refs[2 * n_query : 3 * n_query], refs[3 * n_query]
    slots, width = kept_ref.shape
    tile = last_ref.shape[0]

    @pl.when(step == 0)
    def _():
        bias = [jnp.full((slots, tile), MASKED, jnp.float32) for _ in range(n_query)]
        for s in tile_ids:
            chosen = slots_of(slots, tile, s, info_ref).astype(jnp.float32)
            filled = jnp.max(chosen, axis=1, keepdims=True)
            for q in range(n_query):
                bias[q] = jnp.where(filled > 0.0, mask_row(n_type, q, s, info_ref), bias[q])
        for q in range(n_query):
            bias_ref[:, q * tile : (q + 1) * tile] = bias[q]

    select = slots_of(slots, tile, tile_ids[-1], info_ref).astype(jnp.bfloat16)
    found = jnp.dot(select, last_ref[...], preferred_element_type=jnp.float32)
    kept = (kept_ref[...].astype(jnp.float32) + found).astype(jnp.bfloat16)
    last_mask = jnp.concatenate(
        [mask_row(n_type, q, tile_ids[-1], info_ref) for q in range(n_query)], axis=1
    )
    for head in range(width // HEAD):
        span = slice(head * HEAD, (head + 1) * HEAD)
        scores = product(
            jnp.concatenate([last_ref[:, span], kept[:, span]], axis=0),
            jnp.concatenate([ref[:, span] for ref in query_refs], axis=0),
        )
        last = scores[:tile] + last_mask
        before = jnp.concatenate([ref[head, 8:9] for ref in state_refs], axis=1)
        begun = jnp.concatenate([ref[head, 0:1] for ref in state_refs], axis=1)
        top = jnp.maximum(before, jnp.max(last, axis=0, keepdims=True))
        total = total_of([last], top) + begun * jnp.exp2((before - top) * FACTOR)
        weights = jnp.exp2((scores[tile:] + bias_ref[...] - top) * FACTOR) * (1.0 / total)
        for q in range(n_query):
            out_refs[q][head] = weights[:, q * tile : (q + 1) * tile].astype(jnp.bfloat16)


def weigh_end(n_type, info, kept, last_key, queries, states, tile_ids, first_head, heads):
    tile = last_key.shape[0]
    n_query = len(queries)
    slots = n_type * EXP_CAP
    first = first_head // PER_STEP
    block = pl.BlockSpec((tile, PER_STEP * HEAD), lambda i: (0, i + first))
    state_block = pl.BlockSpec((PER_STEP, 2 * 8, tile), lambda i: (i + first, 0, 0))
    out_block = pl.BlockSpec((PER_STEP, slots, tile), lambda i: (i, 0, 0))
    return pl.pallas_call(
        functools.partial(in_middle, weigh_end_body, n_type, tile_ids),
        grid=(heads // PER_STEP,),
        out_shape=[jax.ShapeDtypeStruct((heads, slots, tile), jnp.bfloat16)] * n_query,
        in_specs=[VMEM, pl.BlockSpec((slots, PER_STEP * HEAD), lambda i: (0, i + first))]
        + [block] * (1 + n_query)
        + [state_block] * n_query,
        out_specs=[out_block] * n_query,
        scratch_shapes=[pltpu.VMEM((slots, n_query * tile), jnp.float32)],
        compiler_params=params(16, dimension_semantics=("arbitrary",)),
        cost_estimate=cost(0, 0),
    )(info, kept, last_key, *queries, *states)


def finish_kernel(n_type, n_part, info_ref, *refs):
    own_refs, back_refs = refs[:n_part], refs[n_part : 2 * n_part]
    values_ref, out_ref, attended_ref, value_ref = refs[2 * n_part :]
    me = lax.axis_index("type")
    ends = (me == 0) | (me == n_type - 1)
    tile = out_ref.shape[0]
    width = out_ref.shape[1]
    for s in range(n_type):
        at = pl.multiple_of(jnp.bitwise_xor(me, s) * EXP_CAP, EXP_CAP)
        value_ref[pl.ds(at, EXP_CAP), :] = values_ref[s * EXP_CAP : (s + 1) * EXP_CAP]
    row = lax.broadcasted_iota(jnp.int32, (n_type * EXP_CAP, tile), 0)
    select = (row == info_ref[0:1, :].astype(jnp.int32)).astype(jnp.bfloat16)
    chunk, count = columns(width)
    contract = (((0,), (0,)), ((), ()))
    for c in range(count):
        span = pl.ds(c * chunk, chunk)
        out_ref[:, span] = lax.dot_general(
            select, value_ref[:, span], contract, preferred_element_type=jnp.float32
        ).astype(jnp.bfloat16)
    at = 0
    for part in range(n_part):
        for h in range(own_refs[part].shape[0]):
            span = pl.ds(at * HEAD, HEAD)
            weights = own_refs[part][h]
            if back_refs:
                weights = jnp.where(ends, back_refs[part][h], weights)
            attended_ref[:, span] = lax.dot_general(
                weights, value_ref[:, span], contract, preferred_element_type=jnp.float32
            ).astype(jnp.bfloat16)
            at += 1


def finish(n_type, info, own, back, values, tile):
    width = values.shape[1]
    n_part = len(own)
    return pl.pallas_call(
        functools.partial(finish_kernel, n_type, n_part),
        out_shape=[jax.ShapeDtypeStruct((tile, width), jnp.bfloat16)] * 2,
        in_specs=[VMEM] * (2 + 2 * n_part),
        out_specs=[VMEM] * 2,
        scratch_shapes=[pltpu.VMEM((n_type * EXP_CAP, width), jnp.bfloat16)],
        compiler_params=params(8),
        cost_estimate=cost(0, 0),
    )(*held([info, *own, *back, values]))


def swap(x, axis, size, s):
    return lax.ppermute(x, axis, [(i, i ^ s) for i in range(size)])


def as_one_step(fn, *operands):
    shapes = jax.eval_shape(fn, *operands)
    blank = lambda *_: jax.tree.map(lambda x: jnp.zeros(x.shape, x.dtype), shapes)
    return lax.cond(lax.axis_index("type") >= 0, fn, blank, *operands)


def on_device(n_dp, n_type, tokens, token_types, tile_mask, queries, keys, gate_weight, up_weight, down_weight):
    tile, width = tokens.shape
    heads = width // HEAD
    tie = lax.optimization_barrier
    n_same = n_dp // 2
    outgoing = route(n_type, token_types.reshape(1, tile), tile_mask.reshape(1, n_type), tokens)
    incoming = [outgoing[0]] + [swap(outgoing[s], "type", n_type, s) for s in range(1, n_type)]

    def experts(incoming, *weights):
        packed, info = pack(n_type, incoming)
        weights = fetch(weights)
        rows = [packed]
        for p in range(1, n_same):
            low = p & -p
            rows.append(swap(rows[p - low], "dp", n_dp, 2 * low))
        rows, weights = tie((rows, weights))
        same_core = jnp.concatenate(rows, axis=0)
        return info, *ffn(same_core, swap(same_core, "dp", n_dp, 1), *weights)

    def gather_sum(own_rows, away_rows, *beside):
        chip_rows = own_rows + swap(away_rows, "dp", n_dp, 1).astype(jnp.float32)
        chip_rows = chip_rows.astype(jnp.bfloat16)
        pieces = [chip_rows[p * EXP_CAP : (p + 1) * EXP_CAP] for p in range(n_same)]
        pieces = [pieces[0]] + [swap(pieces[p], "dp", n_dp, 2 * p) for p in range(1, n_same)]
        begun = None
        if beside:
            info, queries, tiles = beside
            begun = weigh_begin(n_type, info, queries, 0, tiles, [0, 1, 3])
            pieces, begun = tie((pieces, begun))
        total = pieces[0].astype(jnp.float32)
        for piece in pieces[1:]:
            total = total + piece.astype(jnp.float32)
        return total.astype(jnp.bfloat16), begun

    def spread(rows, step=1):
        while step < n_type:
            rows = jnp.concatenate([rows, swap(rows, "type", n_type, step)], axis=0)
            step *= 2
        return rows

    weights = (gate_weight[0], up_weight[0], down_weight[0])
    if n_type == 4:
        to_middle = [(0, 1), (3, 2)]
        across = [(1, 2), (2, 1)]
        to_end = [(1, 0), (2, 3)]
        incoming, keys, queries = tie((incoming, keys, queries))
        near = lax.ppermute(keys, "type", to_middle)
        other = lax.ppermute(keys, "type", across)
        guest = lax.ppermute(queries, "type", to_middle)
        info, own_rows, away_rows = as_one_step(experts, incoming, *weights)
        own_rows, near = tie((own_rows, near))
        far = lax.ppermute(near, "type", across)
        tiles = [keys, near, other]
        expert_rows, (state, kept) = as_one_step(
            gather_sum, own_rows, away_rows, info, queries, tiles
        )
        twin = swap(expert_rows, "type", n_type, 1)
        expert_rows, guest = tie((expert_rows, guest))
        (guest_state,) = weigh_begin(n_type, info, guest, 1, tiles, [0, 1, 3])
        twin, guest_state, far = tie((twin, guest_state, far))
        values = spread(jnp.concatenate([expert_rows, twin], axis=0), 2)
        own_weights, back_weights = [], []
        ends = [0, heads // 2, heads - 8, heads]
        for first, last in zip(ends[:-1], ends[1:]):
            own, theirs = weigh_end(
                n_type,
                info,
                kept,
                far,
                [queries, guest],
                [state, guest_state],
                [0, 1, 3, 2],
                first,
                last - first,
            )
            own_weights.append(own)
            back_weights.append(lax.ppermute(theirs, "type", to_end))
    else:
        info, own_rows, away_rows = experts(incoming, *weights)
        expert_rows, _ = gather_sum(own_rows, away_rows)
        values = spread(expert_rows)
        tiles = [keys] + [swap(keys, "type", n_type, s) for s in range(1, n_type)]
        ids = list(range(n_type))
        state, kept = weigh_begin(n_type, info, queries, 0, tiles[:-1], ids[:-1])
        own_weights = list(
            weigh_end(n_type, info, kept, tiles[-1], [queries], [state], ids, 0, heads)
        )
        back_weights = own_weights
    expert_out, attended = finish(n_type, info, own_weights, back_weights, values, tile)
    return (expert_out, attended)


def solution(mesh):
    return jax.shard_map(
        functools.partial(on_device, mesh.shape["dp"], mesh.shape["type"]),
        mesh=mesh,
        in_specs=(
            P(("dp", "type"), None),
            P(("dp", "type"), None),
            P("dp", "type", None),
            P(("dp", "type"), None),
            P(("dp", "type"), None),
            P("type", None, "dp"),
            P("type", None, "dp"),
            P("type", "dp", None),
        ),
        out_specs=(P(("dp", "type"), None), P(("dp", "type"), None)),
        check_vma=False,
    )
```

```python
import functools
import math

import jax
import jax.numpy as jnp
from jax import lax
from jax.experimental import pallas as pl
from jax.experimental.pallas import tpu as pltpu
from jax.sharding import PartitionSpec as P

HEAD = 128
EXP_CAP = 16
LANES = 128
MASKED = -1e30
MIB = 1024 * 1024
VMEM = pl.BlockSpec(memory_space=pltpu.VMEM)


def params(mib, **more):
    return pltpu.CompilerParams(vmem_limit_bytes=mib * MIB, **more)


def held(arrays):
    return [pltpu.with_memory_space_constraint(x, pltpu.VMEM) for x in arrays]


def cost(flops, bytes_accessed, transcendentals=0):
    return pl.CostEstimate(
        flops=int(flops), bytes_accessed=int(bytes_accessed), transcendentals=int(transcendentals)
    )


def strict_upper(size):
    earlier = lax.broadcasted_iota(jnp.int32, (size, size), 0)
    later = lax.broadcasted_iota(jnp.int32, (size, size), 1)
    return (earlier < later).astype(jnp.bfloat16)


def columns(width):
    for chunk in (1024, 512, 256, 128):
        if width % chunk == 0:
            return chunk, width // chunk
    raise ValueError(width)


def route_kernel(n_type, types_ref, mask_ref, tokens_ref, *refs):
    out_refs, select_ref = refs[:n_type], refs[n_type]
    me = lax.axis_index("type")
    step = pl.program_id(0)
    rows, chunk = tokens_ref.shape
    width = out_refs[0].shape[1] - LANES

    @pl.when(step == 0)
    def _():
        types = types_ref[...]
        hot = lax.broadcasted_iota(jnp.int32, (EXP_CAP, rows), 0) == types
        before = jnp.dot(
            hot.astype(jnp.bfloat16), strict_upper(rows), preferred_element_type=jnp.float32
        )
        rank = jnp.sum(jnp.where(hot, before, 0.0), axis=0, keepdims=True).astype(jnp.int32)
        place = jnp.where(rank < EXP_CAP, jnp.bitwise_xor(types, me) * EXP_CAP + rank, -1)
        select_ref[...] = (
            lax.broadcasted_iota(jnp.int32, (n_type * EXP_CAP, rows), 0) == place
        ).astype(jnp.bfloat16)
        lane = lax.broadcasted_iota(jnp.int32, (EXP_CAP, LANES), 1)
        row = lax.broadcasted_iota(jnp.int32, (EXP_CAP, LANES), 0)
        mask_row = jnp.zeros((EXP_CAP, LANES), jnp.int32)
        for j in range(n_type):
            mask_row = jnp.where(lane == j, mask_ref[0, j], mask_row)
        extra = jnp.where(row == 0, types, jnp.where(row == 1, mask_row, 0))
        extra = extra.astype(jnp.float32).astype(jnp.bfloat16)
        for s in range(n_type):
            out_refs[s][:, pl.ds(width, LANES)] = extra

    moved = jnp.dot(select_ref[...], tokens_ref[...], preferred_element_type=jnp.float32).astype(
        jnp.bfloat16
    )
    span = pl.ds(pl.multiple_of(step * chunk, chunk), chunk)
    for s in range(n_type):
        out_refs[s][:, span] = moved[s * EXP_CAP : (s + 1) * EXP_CAP]


def route(n_type, types, mask_row, tokens):
    rows, width = tokens.shape
    wide = width + LANES
    chunk, count = width // 2, 2
    return pl.pallas_call(
        functools.partial(route_kernel, n_type),
        grid=(count,),
        out_shape=[jax.ShapeDtypeStruct((EXP_CAP, wide), jnp.bfloat16)] * n_type,
        in_specs=[
            VMEM,
            pl.BlockSpec(memory_space=pltpu.SMEM),
            pl.BlockSpec((rows, chunk), lambda i: (0, i)),
        ],
        out_specs=[VMEM] * n_type,
        scratch_shapes=[pltpu.VMEM((n_type * EXP_CAP, rows), jnp.bfloat16)],
        compiler_params=params(8, dimension_semantics=("arbitrary",)),
        cost_estimate=cost(0, 0),
    )(*[pltpu.with_memory_space_constraint(x, pltpu.HBM) for x in (types, mask_row, tokens)])


def fetch_kernel(count, *refs):
    sems = refs[2 * count]
    copies = [pltpu.make_async_copy(refs[i], refs[count + i], sems.at[i]) for i in range(count)]
    for copy in copies:
        copy.start()
    for copy in copies:
        copy.wait()


def fetch(arrays):
    count = len(arrays)
    return pl.pallas_call(
        functools.partial(fetch_kernel, count),
        out_shape=[pltpu.VMEM(x.shape, x.dtype) for x in arrays],
        in_specs=[pl.BlockSpec(memory_space=pl.ANY)] * count,
        out_specs=[VMEM] * count,
        scratch_shapes=[pltpu.SemaphoreType.DMA((count,))],
        compiler_params=params(1),
        cost_estimate=cost(0, 2 * sum(x.size * 2 for x in arrays)),
    )(*[pltpu.with_memory_space_constraint(x, pltpu.HBM) for x in arrays])


def pack_kernel(n_type, *refs):
    in_refs, packed_ref, info_ref = refs[:n_type], refs[n_type], refs[n_type + 1]
    me = lax.axis_index("type")
    width = packed_ref.shape[1]
    tail = pl.ds(width, LANES)
    type_rows = 2 * 8
    row = lax.broadcasted_iota(jnp.int32, (type_rows, LANES), 0)
    upper = strict_upper(LANES)
    extras = [ref[:, tail].astype(jnp.float32) for ref in in_refs]
    types = [e[0:1] for e in extras]
    hots = [row == t.astype(jnp.int32) for t in types]
    befores = [
        jnp.dot(h.astype(jnp.bfloat16), upper, preferred_element_type=jnp.float32) for h in hots
    ]
    counts = [jnp.sum(h.astype(jnp.float32), axis=1, keepdims=True) for h in hots]
    lane16 = lax.broadcasted_iota(jnp.int32, (EXP_CAP, n_type * EXP_CAP), 1)
    slot16 = lax.broadcasted_iota(jnp.int32, (EXP_CAP, n_type * EXP_CAP), 0)
    compact = jnp.zeros((EXP_CAP, n_type * EXP_CAP), jnp.bool_)
    mine = lax.broadcasted_iota(jnp.int32, (type_rows, 1), 0) == me
    info_rows = []
    for s in range(n_type):
        ahead = jnp.zeros((type_rows, 1), jnp.float32)
        for other in range(n_type):
            if other != s:
                first = jnp.bitwise_xor(me, other) < jnp.bitwise_xor(me, s)
                ahead = ahead + jnp.where(first, counts[other], 0.0)
        rank = jnp.sum(jnp.where(hots[s], befores[s] + ahead, 0.0), axis=0, keepdims=True)
        info_rows.append(jnp.where(rank < EXP_CAP, types[s] * EXP_CAP + rank, -1.0))
        offset = jnp.sum(jnp.where(mine, ahead, 0.0)).astype(jnp.int32)
        amount = jnp.sum(jnp.where(mine, counts[s], 0.0)).astype(jnp.int32)
        local = lane16 - s * EXP_CAP
        compact = compact | (
            (local >= 0) & (local < EXP_CAP) & (local < amount) & (local + offset == slot16)
        )
    lane = lax.broadcasted_iota(jnp.int32, (1, LANES), 1)
    for q in range(2):
        for s in range(n_type):
            kept = jnp.sum(
                jnp.where(lane == jnp.bitwise_xor(me, s), extras[q][1:2], 0.0),
                axis=1,
                keepdims=True,
            )
            info_rows.append(jnp.broadcast_to(jnp.where(kept == 1.0, 0.0, MASKED), (1, LANES)))
    for at, info_row in enumerate(info_rows):
        info_ref[at : at + 1, :] = info_row
    compact = compact.astype(jnp.bfloat16)
    chunk, count = columns(width)
    for c in range(count):
        span = pl.ds(c * chunk, chunk)
        rows = jnp.concatenate([ref[:, span] for ref in in_refs], axis=0)
        packed_ref[:, span] = jnp.dot(compact, rows, preferred_element_type=jnp.float32).astype(
            jnp.bfloat16
        )


def pack(n_type, incoming):
    width = incoming[0].shape[1] - LANES
    return pl.pallas_call(
        functools.partial(pack_kernel, n_type),
        out_shape=[
            jax.ShapeDtypeStruct((EXP_CAP, width), jnp.bfloat16),
            jax.ShapeDtypeStruct((3 * n_type, LANES), jnp.float32),
        ],
        in_specs=[VMEM] * n_type,
        out_specs=[VMEM, VMEM],
        compiler_params=params(8),
        cost_estimate=cost(0, 0),
    )(*held(incoming))


def ffn_kernel(near_ref, far_ref, gate_ref, up_ref, down_ref, own_ref, away_ref, x_ref, hidden_ref):
    half = near_ref.shape[0]
    x_ref[:half] = near_ref[...]
    x_ref[half:] = far_ref[...]
    hidden = gate_ref.shape[1]
    for at in range(0, hidden, 256):
        span = pl.ds(at, min(256, hidden - at))
        gate = jnp.dot(x_ref[...], gate_ref[:, span], preferred_element_type=jnp.float32)
        up = jnp.dot(x_ref[...], up_ref[:, span], preferred_element_type=jnp.float32)
        hidden_ref[:, span] = (gate / (1.0 + jnp.exp(-gate)) * up).astype(jnp.bfloat16)
    for at in range(0, down_ref.shape[1], 512):
        span = pl.ds(at, 512)
        out = jnp.dot(hidden_ref[...], down_ref[:, span], preferred_element_type=jnp.float32)
        own_ref[:, span] = out[:half]
        away_ref[:, span] = out[half:].astype(jnp.bfloat16)


def ffn(near, far, gate, up, down):
    half, width = near.shape
    rows = 2 * half
    hidden = gate.shape[1]
    return pl.pallas_call(
        ffn_kernel,
        out_shape=[
            jax.ShapeDtypeStruct((half, width), jnp.float32),
            jax.ShapeDtypeStruct((half, width), jnp.bfloat16),
        ],
        in_specs=[VMEM] * 5,
        out_specs=[VMEM] * 2,
        scratch_shapes=[
            pltpu.VMEM((rows, width), jnp.bfloat16),
            pltpu.VMEM((rows, hidden), jnp.bfloat16),
        ],
        compiler_params=params(16),
        cost_estimate=cost(0, 0),
    )(*held([near, far, gate, up, down]))


FACTOR = math.log2(math.e) / math.sqrt(HEAD)


def slots_of(slots, tile, s, info_ref):
    row = lax.broadcasted_iota(jnp.int32, (slots, tile), 0)
    return row == info_ref[s : s + 1, :].astype(jnp.int32)


def mask_row(n_type, q, s, info_ref):
    line = (1 + q) * n_type + s
    return info_ref[line : line + 1, :]


def product(rows, queries):
    return lax.dot_general(
        rows, queries, (((1,), (1,)), ((), ())), preferred_element_type=jnp.float32
    )


def pair_of(query):
    lane = lax.broadcasted_iota(jnp.int32, query.shape, 1)
    zero = jnp.zeros_like(query)
    return jnp.concatenate(
        [jnp.where(lane < HEAD, query, zero), jnp.where(lane >= HEAD, query, zero)], axis=0
    )


def pair_scores(n_type, q, tile_ids, info_ref, key_refs, query_ref, span):
    tile = query_ref.shape[0]
    scores = product(
        jnp.concatenate([ref[:, span] for ref in key_refs], axis=0), pair_of(query_ref[:, span])
    )
    scores = [scores[i * tile : (i + 1) * tile] for i in range(len(tile_ids))]
    masks = [mask_row(n_type, q, s, info_ref) for s in tile_ids]
    return [x + jnp.concatenate([m, m], axis=1) for x, m in zip(scores, masks)]


def top_of(scores):
    return functools.reduce(jnp.maximum, [jnp.max(x, axis=0, keepdims=True) for x in scores])


def total_of(scores, top):
    return sum(jnp.sum(jnp.exp2((x - top) * FACTOR), axis=0, keepdims=True) for x in scores)


def in_middle(body, n_type, *args):
    me = lax.axis_index("type")
    step = pl.program_id(0)
    if n_type != 4:
        body(step, n_type, *args)
    else:

        @pl.when((me > 0) & (me < n_type - 1))
        def _():
            body(step, n_type, *args)


def weigh_begin_body(step, n_type, tile_ids, query_id, info_ref, query_ref, *refs):
    key_refs = refs[: len(tile_ids)]
    state_ref, *kept_refs = refs[len(tile_ids) :]
    tile, width = query_ref.shape
    for kept_ref in kept_refs:
        slots = kept_ref.shape[0]
        select = [slots_of(slots, tile, s, info_ref).astype(jnp.bfloat16) for s in tile_ids]
        kept_ref[...] = jnp.dot(
            jnp.concatenate(select, axis=1),
            jnp.concatenate([ref[...] for ref in key_refs], axis=0),
            preferred_element_type=jnp.float32,
        ).astype(jnp.bfloat16)
    for at in range(0, width, 2 * HEAD):
        span = pl.ds(at, 2 * HEAD)
        scores = pair_scores(n_type, query_id, tile_ids, info_ref, key_refs, query_ref, span)
        top = top_of(scores)
        total = total_of(scores, top)
        for i in range(2):
            mine = slice(i * tile, (i + 1) * tile)
            head = at // HEAD + i
            state_ref[head, :8] = jnp.broadcast_to(total[:, mine], (8, tile))
            state_ref[head, 8:] = jnp.broadcast_to(top[:, mine], (8, tile))


PER_STEP = 16


def weigh_begin(n_type, info, query, query_id, keys, tile_ids):
    tile, width = query.shape
    heads = width // HEAD
    slots = n_type * EXP_CAP
    block = pl.BlockSpec((tile, PER_STEP * HEAD), lambda i: (0, i))
    return pl.pallas_call(
        functools.partial(in_middle, weigh_begin_body, n_type, tile_ids, query_id),
        grid=(heads // PER_STEP,),
        out_shape=[
            jax.ShapeDtypeStruct((heads, 2 * 8, tile), jnp.float32),
            jax.ShapeDtypeStruct((slots, width), jnp.bfloat16),
        ][: 2 - query_id],
        in_specs=[VMEM] + [block] * (1 + len(keys)),
        out_specs=[
            pl.BlockSpec((PER_STEP, 2 * 8, tile), lambda i: (i, 0, 0)),
            pl.BlockSpec((slots, PER_STEP * HEAD), lambda i: (0, i)),
        ][: 2 - query_id],
        compiler_params=params(16, dimension_semantics=("arbitrary",)),
        cost_estimate=cost(0, 16 * tile * tile * heads),
    )(info, query, *keys)


def weigh_end_body(step, n_type, tile_ids, info_ref, kept_ref, last_ref, *refs):
    n_query = (len(refs) - 1) // 3
    query_refs, state_refs = refs[:n_query], refs[n_query : 2 * n_query]
    out_refs, bias_ref = refs[2 * n_query : 3 * n_query], refs[3 * n_query]
    slots, width = kept_ref.shape
    tile = last_ref.shape[0]

    @pl.when(step == 0)
    def _():
        bias = [jnp.full((slots, tile), MASKED, jnp.float32) for _ in range(n_query)]
        for s in tile_ids:
            chosen = slots_of(slots, tile, s, info_ref).astype(jnp.float32)
            filled = jnp.max(chosen, axis=1, keepdims=True)
            for q in range(n_query):
                bias[q] = jnp.where(filled > 0.0, mask_row(n_type, q, s, info_ref), bias[q])
        for q in range(n_query):
            bias_ref[:, q * tile : (q + 1) * tile] = bias[q]

    select = slots_of(slots, tile, tile_ids[-1], info_ref).astype(jnp.bfloat16)
    found = jnp.dot(select, last_ref[...], preferred_element_type=jnp.float32)
    kept = (kept_ref[...].astype(jnp.float32) + found).astype(jnp.bfloat16)
    last_mask = jnp.concatenate(
        [mask_row(n_type, q, tile_ids[-1], info_ref) for q in range(n_query)], axis=1
    )
    for head in range(width // HEAD):
        span = slice(head * HEAD, (head + 1) * HEAD)
        scores = product(
            jnp.concatenate([last_ref[:, span], kept[:, span]], axis=0),
            jnp.concatenate([ref[:, span] for ref in query_refs], axis=0),
        )
        last = scores[:tile] + last_mask
        before = jnp.concatenate([ref[head, 8:9] for ref in state_refs], axis=1)
        begun = jnp.concatenate([ref[head, 0:1] for ref in state_refs], axis=1)
        top = jnp.maximum(before, jnp.max(last, axis=0, keepdims=True))
        total = total_of([last], top) + begun * jnp.exp2((before - top) * FACTOR)
        weights = jnp.exp2((scores[tile:] + bias_ref[...] - top) * FACTOR) * (1.0 / total)
        for q in range(n_query):
            out_refs[q][head] = weights[:, q * tile : (q + 1) * tile].astype(jnp.bfloat16)


def weigh_end(n_type, info, kept, last_key, queries, states, tile_ids, first_head, heads, weight=0):
    tile = last_key.shape[0]
    n_query = len(queries)
    slots = n_type * EXP_CAP
    first = first_head // PER_STEP
    block = pl.BlockSpec((tile, PER_STEP * HEAD), lambda i: (0, i + first))
    state_block = pl.BlockSpec((PER_STEP, 2 * 8, tile), lambda i: (i + first, 0, 0))
    out_block = pl.BlockSpec((PER_STEP, slots, tile), lambda i: (i, 0, 0))
    return pl.pallas_call(
        functools.partial(in_middle, weigh_end_body, n_type, tile_ids),
        grid=(heads // PER_STEP,),
        out_shape=[jax.ShapeDtypeStruct((heads, slots, tile), jnp.bfloat16)] * n_query,
        in_specs=[VMEM, pl.BlockSpec((slots, PER_STEP * HEAD), lambda i: (0, i + first))]
        + [block] * (1 + n_query)
        + [state_block] * n_query,
        out_specs=[out_block] * n_query,
        scratch_shapes=[pltpu.VMEM((slots, n_query * tile), jnp.float32)],
        compiler_params=params(16, dimension_semantics=("arbitrary",)),
        cost_estimate=cost(0, weight),
    )(info, kept, last_key, *queries, *states)


def finish_kernel(n_type, n_part, info_ref, *refs):
    own_refs, back_refs = refs[:n_part], refs[n_part : 2 * n_part]
    values_ref, out_ref, attended_ref, value_ref = refs[2 * n_part :]
    me = lax.axis_index("type")
    ends = (me == 0) | (me == n_type - 1)
    tile = out_ref.shape[0]
    width = out_ref.shape[1]
    for s in range(n_type):
        at = pl.multiple_of(jnp.bitwise_xor(me, s) * EXP_CAP, EXP_CAP)
        value_ref[pl.ds(at, EXP_CAP), :] = values_ref[s * EXP_CAP : (s + 1) * EXP_CAP]
    row = lax.broadcasted_iota(jnp.int32, (n_type * EXP_CAP, tile), 0)
    select = (row == info_ref[0:1, :].astype(jnp.int32)).astype(jnp.bfloat16)
    chunk, count = columns(width)
    contract = (((0,), (0,)), ((), ()))
    for c in range(count):
        span = pl.ds(c * chunk, chunk)
        out_ref[:, span] = lax.dot_general(
            select, value_ref[:, span], contract, preferred_element_type=jnp.float32
        ).astype(jnp.bfloat16)
    at = 0
    for part in range(n_part):
        for h in range(own_refs[part].shape[0]):
            span = pl.ds(at * HEAD, HEAD)
            weights = own_refs[part][h]
            if back_refs:
                weights = jnp.where(ends, back_refs[part][h], weights)
            attended_ref[:, span] = lax.dot_general(
                weights, value_ref[:, span], contract, preferred_element_type=jnp.float32
            ).astype(jnp.bfloat16)
            at += 1


def finish(n_type, info, own, back, values, tile):
    width = values.shape[1]
    n_part = len(own)
    return pl.pallas_call(
        functools.partial(finish_kernel, n_type, n_part),
        out_shape=[jax.ShapeDtypeStruct((tile, width), jnp.bfloat16)] * 2,
        in_specs=[VMEM] * (2 + 2 * n_part),
        out_specs=[VMEM] * 2,
        scratch_shapes=[pltpu.VMEM((n_type * EXP_CAP, width), jnp.bfloat16)],
        compiler_params=params(8),
        cost_estimate=cost(0, 0),
    )(*held([info, *own, *back, values]))


def swap(x, axis, size, s):
    return lax.ppermute(x, axis, [(i, i ^ s) for i in range(size)])


def as_one_step(fn, *operands):
    shapes = jax.eval_shape(fn, *operands)
    blank = lambda *_: jax.tree.map(lambda x: jnp.zeros(x.shape, x.dtype), shapes)
    return lax.cond(lax.axis_index("type") >= 0, fn, blank, *operands)


def on_device(n_dp, n_type, tokens, token_types, tile_mask, queries, keys, gate_weight, up_weight, down_weight):
    tile, width = tokens.shape
    heads = width // HEAD
    tie = lax.optimization_barrier
    n_same = n_dp // 2
    outgoing = route(n_type, token_types.reshape(1, tile), tile_mask.reshape(1, n_type), tokens)
    incoming = [outgoing[0]] + [swap(outgoing[s], "type", n_type, s) for s in range(1, n_type)]

    def experts(incoming, *weights):
        packed, info = pack(n_type, incoming)
        weights = fetch(weights)
        rows = [packed]
        for p in range(1, n_same):
            low = p & -p
            rows.append(swap(rows[p - low], "dp", n_dp, 2 * low))
        rows, weights = tie((rows, weights))
        same_core = jnp.concatenate(rows, axis=0)
        return info, *ffn(same_core, swap(same_core, "dp", n_dp, 1), *weights)

    def gather_sum(own_rows, away_rows, *beside):
        chip_rows = own_rows + swap(away_rows, "dp", n_dp, 1).astype(jnp.float32)
        chip_rows = chip_rows.astype(jnp.bfloat16)
        pieces = [chip_rows[p * EXP_CAP : (p + 1) * EXP_CAP] for p in range(n_same)]
        pieces = [pieces[0]] + [swap(pieces[p], "dp", n_dp, 2 * p) for p in range(1, n_same)]
        begun = None
        if beside:
            info, queries, tiles = beside
            begun = weigh_begin(n_type, info, queries, 0, tiles, [0, 1, 3])
            pieces, begun = tie((pieces, begun))
        total = pieces[0].astype(jnp.float32)
        for piece in pieces[1:]:
            total = total + piece.astype(jnp.float32)
        return total.astype(jnp.bfloat16), begun

    def spread(rows, step=1):
        while step < n_type:
            rows = jnp.concatenate([rows, swap(rows, "type", n_type, step)], axis=0)
            step *= 2
        return rows

    weights = (gate_weight[0], up_weight[0], down_weight[0])
    if n_type == 4:
        to_middle = [(0, 1), (3, 2)]
        across = [(1, 2), (2, 1)]
        to_end = [(1, 0), (2, 3)]
        incoming, keys, queries = tie((incoming, keys, queries))
        near = lax.ppermute(keys, "type", to_middle)
        other = lax.ppermute(keys, "type", across)
        guest = lax.ppermute(queries, "type", to_middle)
        info, own_rows, away_rows = as_one_step(experts, incoming, *weights)
        own_rows, near = tie((own_rows, near))
        far = lax.ppermute(near, "type", across)
        tiles = [keys, near, other]
        expert_rows, (state, kept) = as_one_step(
            gather_sum, own_rows, away_rows, info, queries, tiles
        )
        twin = swap(expert_rows, "type", n_type, 1)
        expert_rows, guest = tie((expert_rows, guest))
        (guest_state,) = weigh_begin(n_type, info, guest, 1, tiles, [0, 1, 3])
        twin, guest_state, far = tie((twin, guest_state, far))
        values = spread(jnp.concatenate([expert_rows, twin], axis=0), 2)
        own_weights, back_weights = [], []
        ends = [0, heads // 2, heads]
        for first, last in zip(ends[:-1], ends[1:]):
            own, theirs = weigh_end(
                n_type,
                info,
                kept,
                far,
                [queries, guest],
                [state, guest_state],
                [0, 1, 3, 2],
                first,
                last - first,
                (1 << 30) if first > 0 else 0,
            )
            own_weights.append(own)
            back_weights.append(lax.ppermute(theirs, "type", to_end))
    else:
        info, own_rows, away_rows = experts(incoming, *weights)
        expert_rows, _ = gather_sum(own_rows, away_rows)
        values = spread(expert_rows)
        tiles = [keys] + [swap(keys, "type", n_type, s) for s in range(1, n_type)]
        ids = list(range(n_type))
        state, kept = weigh_begin(n_type, info, queries, 0, tiles[:-1], ids[:-1])
        own_weights = list(
            weigh_end(n_type, info, kept, tiles[-1], [queries], [state], ids, 0, heads)
        )
        back_weights = own_weights
    expert_out, attended = finish(n_type, info, own_weights, back_weights, values, tile)
    return (expert_out, attended)


def solution(mesh):
    return jax.shard_map(
        functools.partial(on_device, mesh.shape["dp"], mesh.shape["type"]),
        mesh=mesh,
        in_specs=(
            P(("dp", "type"), None),
            P(("dp", "type"), None),
            P("dp", "type", None),
            P(("dp", "type"), None),
            P(("dp", "type"), None),
            P("type", None, "dp"),
            P("type", None, "dp"),
            P("type", "dp", None),
        ),
        out_specs=(P(("dp", "type"), None), P(("dp", "type"), None)),
        check_vma=False,
    )
```

```python
import functools
import math

import jax
import jax.numpy as jnp
from jax import lax
from jax.experimental import pallas as pl
from jax.experimental.pallas import tpu as pltpu
from jax.sharding import PartitionSpec as P

HEAD = 128
EXP_CAP = 16
LANES = 128
MASKED = -1e30
MIB = 1024 * 1024
VMEM = pl.BlockSpec(memory_space=pltpu.VMEM)


def params(mib, **more):
    return pltpu.CompilerParams(vmem_limit_bytes=mib * MIB, **more)


def held(arrays):
    return [pltpu.with_memory_space_constraint(x, pltpu.VMEM) for x in arrays]


def cost(flops, bytes_accessed, transcendentals=0):
    return pl.CostEstimate(
        flops=int(flops), bytes_accessed=int(bytes_accessed), transcendentals=int(transcendentals)
    )


def strict_upper(size):
    earlier = lax.broadcasted_iota(jnp.int32, (size, size), 0)
    later = lax.broadcasted_iota(jnp.int32, (size, size), 1)
    return (earlier < later).astype(jnp.bfloat16)


def columns(width):
    for chunk in (1024, 512, 256, 128):
        if width % chunk == 0:
            return chunk, width // chunk
    raise ValueError(width)


def route_kernel(n_type, types_ref, mask_ref, tokens_ref, *refs):
    out_refs, select_ref = refs[:n_type], refs[n_type]
    me = lax.axis_index("type")
    step = pl.program_id(0)
    rows, chunk = tokens_ref.shape
    width = out_refs[0].shape[1] - LANES

    @pl.when(step == 0)
    def _():
        types = types_ref[...]
        hot = lax.broadcasted_iota(jnp.int32, (EXP_CAP, rows), 0) == types
        before = jnp.dot(
            hot.astype(jnp.bfloat16), strict_upper(rows), preferred_element_type=jnp.float32
        )
        rank = jnp.sum(jnp.where(hot, before, 0.0), axis=0, keepdims=True).astype(jnp.int32)
        place = jnp.where(rank < EXP_CAP, jnp.bitwise_xor(types, me) * EXP_CAP + rank, -1)
        select_ref[...] = (
            lax.broadcasted_iota(jnp.int32, (n_type * EXP_CAP, rows), 0) == place
        ).astype(jnp.bfloat16)
        lane = lax.broadcasted_iota(jnp.int32, (EXP_CAP, LANES), 1)
        row = lax.broadcasted_iota(jnp.int32, (EXP_CAP, LANES), 0)
        mask_row = jnp.zeros((EXP_CAP, LANES), jnp.int32)
        for j in range(n_type):
            mask_row = jnp.where(lane == j, mask_ref[0, j], mask_row)
        extra = jnp.where(row == 0, types, jnp.where(row == 1, mask_row, 0))
        extra = extra.astype(jnp.float32).astype(jnp.bfloat16)
        for s in range(n_type):
            out_refs[s][:, pl.ds(width, LANES)] = extra

    moved = jnp.dot(select_ref[...], tokens_ref[...], preferred_element_type=jnp.float32).astype(
        jnp.bfloat16
    )
    span = pl.ds(pl.multiple_of(step * chunk, chunk), chunk)
    for s in range(n_type):
        out_refs[s][:, span] = moved[s * EXP_CAP : (s + 1) * EXP_CAP]


def route(n_type, types, mask_row, tokens):
    rows, width = tokens.shape
    wide = width + LANES
    chunk, count = width // 2, 2
    return pl.pallas_call(
        functools.partial(route_kernel, n_type),
        grid=(count,),
        out_shape=[jax.ShapeDtypeStruct((EXP_CAP, wide), jnp.bfloat16)] * n_type,
        in_specs=[
            VMEM,
            pl.BlockSpec(memory_space=pltpu.SMEM),
            pl.BlockSpec((rows, chunk), lambda i: (0, i)),
        ],
        out_specs=[VMEM] * n_type,
        scratch_shapes=[pltpu.VMEM((n_type * EXP_CAP, rows), jnp.bfloat16)],
        compiler_params=params(8, dimension_semantics=("arbitrary",)),
        cost_estimate=cost(0, 0),
    )(*[pltpu.with_memory_space_constraint(x, pltpu.HBM) for x in (types, mask_row, tokens)])


def fetch_kernel(count, *refs):
    sems = refs[2 * count]
    copies = [pltpu.make_async_copy(refs[i], refs[count + i], sems.at[i]) for i in range(count)]
    for copy in copies:
        copy.start()
    for copy in copies:
        copy.wait()


def fetch(arrays):
    count = len(arrays)
    return pl.pallas_call(
        functools.partial(fetch_kernel, count),
        out_shape=[pltpu.VMEM(x.shape, x.dtype) for x in arrays],
        in_specs=[pl.BlockSpec(memory_space=pl.ANY)] * count,
        out_specs=[VMEM] * count,
        scratch_shapes=[pltpu.SemaphoreType.DMA((count,))],
        compiler_params=params(1),
        cost_estimate=cost(0, 2 * sum(x.size * 2 for x in arrays)),
    )(*[pltpu.with_memory_space_constraint(x, pltpu.HBM) for x in arrays])


def pack_kernel(n_type, *refs):
    in_refs, packed_ref, info_ref = refs[:n_type], refs[n_type], refs[n_type + 1]
    me = lax.axis_index("type")
    width = packed_ref.shape[1]
    tail = pl.ds(width, LANES)
    type_rows = 2 * 8
    row = lax.broadcasted_iota(jnp.int32, (type_rows, LANES), 0)
    upper = strict_upper(LANES)
    extras = [ref[:, tail].astype(jnp.float32) for ref in in_refs]
    types = [e[0:1] for e in extras]
    hots = [row == t.astype(jnp.int32) for t in types]
    befores = [
        jnp.dot(h.astype(jnp.bfloat16), upper, preferred_element_type=jnp.float32) for h in hots
    ]
    counts = [jnp.sum(h.astype(jnp.float32), axis=1, keepdims=True) for h in hots]
    lane16 = lax.broadcasted_iota(jnp.int32, (EXP_CAP, n_type * EXP_CAP), 1)
    slot16 = lax.broadcasted_iota(jnp.int32, (EXP_CAP, n_type * EXP_CAP), 0)
    compact = jnp.zeros((EXP_CAP, n_type * EXP_CAP), jnp.bool_)
    mine = lax.broadcasted_iota(jnp.int32, (type_rows, 1), 0) == me
    info_rows = []
    for s in range(n_type):
        ahead = jnp.zeros((type_rows, 1), jnp.float32)
        for other in range(n_type):
            if other != s:
                first = jnp.bitwise_xor(me, other) < jnp.bitwise_xor(me, s)
                ahead = ahead + jnp.where(first, counts[other], 0.0)
        rank = jnp.sum(jnp.where(hots[s], befores[s] + ahead, 0.0), axis=0, keepdims=True)
        info_rows.append(jnp.where(rank < EXP_CAP, types[s] * EXP_CAP + rank, -1.0))
        offset = jnp.sum(jnp.where(mine, ahead, 0.0)).astype(jnp.int32)
        amount = jnp.sum(jnp.where(mine, counts[s], 0.0)).astype(jnp.int32)
        local = lane16 - s * EXP_CAP
        compact = compact | (
            (local >= 0) & (local < EXP_CAP) & (local < amount) & (local + offset == slot16)
        )
    lane = lax.broadcasted_iota(jnp.int32, (1, LANES), 1)
    for q in range(2):
        for s in range(n_type):
            kept = jnp.sum(
                jnp.where(lane == jnp.bitwise_xor(me, s), extras[q][1:2], 0.0),
                axis=1,
                keepdims=True,
            )
            info_rows.append(jnp.broadcast_to(jnp.where(kept == 1.0, 0.0, MASKED), (1, LANES)))
    for at, info_row in enumerate(info_rows):
        info_ref[at : at + 1, :] = info_row
    compact = compact.astype(jnp.bfloat16)
    chunk, count = columns(width)
    for c in range(count):
        span = pl.ds(c * chunk, chunk)
        rows = jnp.concatenate([ref[:, span] for ref in in_refs], axis=0)
        packed_ref[:, span] = jnp.dot(compact, rows, preferred_element_type=jnp.float32).astype(
            jnp.bfloat16
        )


def pack(n_type, incoming):
    width = incoming[0].shape[1] - LANES
    return pl.pallas_call(
        functools.partial(pack_kernel, n_type),
        out_shape=[
            jax.ShapeDtypeStruct((EXP_CAP, width), jnp.bfloat16),
            jax.ShapeDtypeStruct((3 * n_type, LANES), jnp.float32),
        ],
        in_specs=[VMEM] * n_type,
        out_specs=[VMEM, VMEM],
        compiler_params=params(8),
        cost_estimate=cost(0, 0),
    )(*held(incoming))


def ffn_kernel(near_ref, far_ref, gate_ref, up_ref, down_ref, own_ref, away_ref, x_ref, hidden_ref):
    half = near_ref.shape[0]
    x_ref[:half] = near_ref[...]
    x_ref[half:] = far_ref[...]
    hidden = gate_ref.shape[1]
    for at in range(0, hidden, 256):
        span = pl.ds(at, min(256, hidden - at))
        gate = jnp.dot(x_ref[...], gate_ref[:, span], preferred_element_type=jnp.float32)
        up = jnp.dot(x_ref[...], up_ref[:, span], preferred_element_type=jnp.float32)
        hidden_ref[:, span] = (gate / (1.0 + jnp.exp(-gate)) * up).astype(jnp.bfloat16)
    for at in range(0, down_ref.shape[1], 512):
        span = pl.ds(at, 512)
        out = jnp.dot(hidden_ref[...], down_ref[:, span], preferred_element_type=jnp.float32)
        own_ref[:, span] = out[:half]
        away_ref[:, span] = out[half:].astype(jnp.bfloat16)


def ffn(near, far, gate, up, down):
    half, width = near.shape
    rows = 2 * half
    hidden = gate.shape[1]
    return pl.pallas_call(
        ffn_kernel,
        out_shape=[
            jax.ShapeDtypeStruct((half, width), jnp.float32),
            jax.ShapeDtypeStruct((half, width), jnp.bfloat16),
        ],
        in_specs=[VMEM] * 5,
        out_specs=[VMEM] * 2,
        scratch_shapes=[
            pltpu.VMEM((rows, width), jnp.bfloat16),
            pltpu.VMEM((rows, hidden), jnp.bfloat16),
        ],
        compiler_params=params(16),
        cost_estimate=cost(0, 0),
    )(*held([near, far, gate, up, down]))


FACTOR = math.log2(math.e) / math.sqrt(HEAD)


def slots_of(slots, tile, s, info_ref):
    row = lax.broadcasted_iota(jnp.int32, (slots, tile), 0)
    return row == info_ref[s : s + 1, :].astype(jnp.int32)


def mask_row(n_type, q, s, info_ref):
    line = (1 + q) * n_type + s
    return info_ref[line : line + 1, :]


def product(rows, queries):
    return lax.dot_general(
        rows, queries, (((1,), (1,)), ((), ())), preferred_element_type=jnp.float32
    )


def pair_of(query):
    lane = lax.broadcasted_iota(jnp.int32, query.shape, 1)
    zero = jnp.zeros_like(query)
    return jnp.concatenate(
        [jnp.where(lane < HEAD, query, zero), jnp.where(lane >= HEAD, query, zero)], axis=0
    )


def pair_scores(n_type, q, tile_ids, info_ref, key_refs, query_ref, span):
    tile = query_ref.shape[0]
    scores = product(
        jnp.concatenate([ref[:, span] for ref in key_refs], axis=0), pair_of(query_ref[:, span])
    )
    scores = [scores[i * tile : (i + 1) * tile] for i in range(len(tile_ids))]
    masks = [mask_row(n_type, q, s, info_ref) for s in tile_ids]
    return [x + jnp.concatenate([m, m], axis=1) for x, m in zip(scores, masks)]


def top_of(scores):
    return functools.reduce(jnp.maximum, [jnp.max(x, axis=0, keepdims=True) for x in scores])


def total_of(scores, top):
    return sum(jnp.sum(jnp.exp2((x - top) * FACTOR), axis=0, keepdims=True) for x in scores)


def in_middle(body, n_type, *args):
    me = lax.axis_index("type")
    step = pl.program_id(0)
    if n_type != 4:
        body(step, n_type, *args)
    else:

        @pl.when((me > 0) & (me < n_type - 1))
        def _():
            body(step, n_type, *args)


def weigh_begin_body(step, n_type, tile_ids, query_id, info_ref, query_ref, *refs):
    key_refs = refs[: len(tile_ids)]
    state_ref, *kept_refs = refs[len(tile_ids) :]
    tile, width = query_ref.shape
    for kept_ref in kept_refs:
        slots = kept_ref.shape[0]
        select = [slots_of(slots, tile, s, info_ref).astype(jnp.bfloat16) for s in tile_ids]
        kept_ref[...] = jnp.dot(
            jnp.concatenate(select, axis=1),
            jnp.concatenate([ref[...] for ref in key_refs], axis=0),
            preferred_element_type=jnp.float32,
        ).astype(jnp.bfloat16)
    for at in range(0, width, 2 * HEAD):
        span = pl.ds(at, 2 * HEAD)
        scores = pair_scores(n_type, query_id, tile_ids, info_ref, key_refs, query_ref, span)
        top = top_of(scores)
        total = total_of(scores, top)
        for i in range(2):
            mine = slice(i * tile, (i + 1) * tile)
            head = at // HEAD + i
            state_ref[head, :8] = jnp.broadcast_to(total[:, mine], (8, tile))
            state_ref[head, 8:] = jnp.broadcast_to(top[:, mine], (8, tile))


PER_STEP = 16


def weigh_begin(n_type, info, query, query_id, keys, tile_ids):
    tile, width = query.shape
    heads = width // HEAD
    slots = n_type * EXP_CAP
    block = pl.BlockSpec((tile, PER_STEP * HEAD), lambda i: (0, i))
    return pl.pallas_call(
        functools.partial(in_middle, weigh_begin_body, n_type, tile_ids, query_id),
        grid=(heads // PER_STEP,),
        out_shape=[
            jax.ShapeDtypeStruct((heads, 2 * 8, tile), jnp.float32),
            jax.ShapeDtypeStruct((slots, width), jnp.bfloat16),
        ][: 2 - query_id],
        in_specs=[VMEM] + [block] * (1 + len(keys)),
        out_specs=[
            pl.BlockSpec((PER_STEP, 2 * 8, tile), lambda i: (i, 0, 0)),
            pl.BlockSpec((slots, PER_STEP * HEAD), lambda i: (0, i)),
        ][: 2 - query_id],
        compiler_params=params(16, dimension_semantics=("arbitrary",)),
        cost_estimate=cost(0, 16 * tile * tile * heads),
    )(info, query, *keys)


def weigh_end_body(step, n_type, tile_ids, info_ref, kept_ref, last_ref, *refs):
    n_query = (len(refs) - 1) // 3
    query_refs, state_refs = refs[:n_query], refs[n_query : 2 * n_query]
    out_refs, bias_ref = refs[2 * n_query : 3 * n_query], refs[3 * n_query]
    slots, width = kept_ref.shape
    tile = last_ref.shape[0]

    @pl.when(step == 0)
    def _():
        bias = [jnp.full((slots, tile), MASKED, jnp.float32) for _ in range(n_query)]
        for s in tile_ids:
            chosen = slots_of(slots, tile, s, info_ref).astype(jnp.float32)
            filled = jnp.max(chosen, axis=1, keepdims=True)
            for q in range(n_query):
                bias[q] = jnp.where(filled > 0.0, mask_row(n_type, q, s, info_ref), bias[q])
        for q in range(n_query):
            bias_ref[:, q * tile : (q + 1) * tile] = bias[q]

    select = slots_of(slots, tile, tile_ids[-1], info_ref).astype(jnp.bfloat16)
    found = jnp.dot(select, last_ref[...], preferred_element_type=jnp.float32)
    kept = (kept_ref[...].astype(jnp.float32) + found).astype(jnp.bfloat16)
    last_mask = jnp.concatenate(
        [mask_row(n_type, q, tile_ids[-1], info_ref) for q in range(n_query)], axis=1
    )
    for head in range(width // HEAD):
        span = slice(head * HEAD, (head + 1) * HEAD)
        scores = product(
            jnp.concatenate([last_ref[:, span], kept[:, span]], axis=0),
            jnp.concatenate([ref[:, span] for ref in query_refs], axis=0),
        )
        last = scores[:tile] + last_mask
        before = jnp.concatenate([ref[head, 8:9] for ref in state_refs], axis=1)
        begun = jnp.concatenate([ref[head, 0:1] for ref in state_refs], axis=1)
        top = jnp.maximum(before, jnp.max(last, axis=0, keepdims=True))
        total = total_of([last], top) + begun * jnp.exp2((before - top) * FACTOR)
        weights = jnp.exp2((scores[tile:] + bias_ref[...] - top) * FACTOR) * (1.0 / total)
        for q in range(n_query):
            out_refs[q][head] = weights[:, q * tile : (q + 1) * tile].astype(jnp.bfloat16)


def weigh_end(n_type, info, kept, last_key, queries, states, tile_ids, first_head, heads, weight=0):
    tile = last_key.shape[0]
    n_query = len(queries)
    slots = n_type * EXP_CAP
    first = first_head // PER_STEP
    block = pl.BlockSpec((tile, PER_STEP * HEAD), lambda i: (0, i + first))
    state_block = pl.BlockSpec((PER_STEP, 2 * 8, tile), lambda i: (i + first, 0, 0))
    out_block = pl.BlockSpec((PER_STEP, slots, tile), lambda i: (i, 0, 0))
    return pl.pallas_call(
        functools.partial(in_middle, weigh_end_body, n_type, tile_ids),
        grid=(heads // PER_STEP,),
        out_shape=[jax.ShapeDtypeStruct((heads, slots, tile), jnp.bfloat16)] * n_query,
        in_specs=[VMEM, pl.BlockSpec((slots, PER_STEP * HEAD), lambda i: (0, i + first))]
        + [block] * (1 + n_query)
        + [state_block] * n_query,
        out_specs=[out_block] * n_query,
        scratch_shapes=[pltpu.VMEM((slots, n_query * tile), jnp.float32)],
        compiler_params=params(16, dimension_semantics=("arbitrary",)),
        cost_estimate=cost(0, weight),
    )(info, kept, last_key, *queries, *states)


def by_expert(n_type, values_ref, value_ref):
    me = lax.axis_index("type")
    for s in range(n_type):
        at = pl.multiple_of(jnp.bitwise_xor(me, s) * EXP_CAP, EXP_CAP)
        value_ref[pl.ds(at, EXP_CAP), :] = values_ref[s * EXP_CAP : (s + 1) * EXP_CAP]


CONTRACT = (((0,), (0,)), ((), ()))


def expert_out_kernel(n_type, info_ref, values_ref, out_ref, value_ref):
    tile, width = out_ref.shape
    by_expert(n_type, values_ref, value_ref)
    select = slots_of(n_type * EXP_CAP, tile, 0, info_ref).astype(jnp.bfloat16)
    chunk, count = columns(width)
    for c in range(count):
        span = pl.ds(c * chunk, chunk)
        out_ref[:, span] = lax.dot_general(
            select, value_ref[:, span], CONTRACT, preferred_element_type=jnp.float32
        ).astype(jnp.bfloat16)


def expert_output(n_type, info, values, tile):
    slots, width = values.shape
    return pl.pallas_call(
        functools.partial(expert_out_kernel, n_type),
        out_shape=jax.ShapeDtypeStruct((tile, width), jnp.bfloat16),
        in_specs=[VMEM] * 2,
        out_specs=VMEM,
        scratch_shapes=[pltpu.VMEM((slots, width), jnp.bfloat16)],
        compiler_params=params(8),
        cost_estimate=cost(0, 0),
    )(*held([info, values]))


def attend_kernel(n_type, n_part, values_ref, *refs):
    own_refs, back_refs = refs[:n_part], refs[n_part : 2 * n_part]
    result_ref, value_ref, attended_ref, sems = refs[2 * n_part :]
    me = lax.axis_index("type")
    ends = (me == 0) | (me == n_type - 1)
    by_expert(n_type, values_ref, value_ref)
    at = 0
    copies = []
    for part in range(n_part):
        for h in range(own_refs[part].shape[0]):
            span = pl.ds(at * HEAD, HEAD)
            weights = jnp.where(ends, back_refs[part][h], own_refs[part][h])
            attended_ref[:, span] = lax.dot_general(
                weights, value_ref[:, span], CONTRACT, preferred_element_type=jnp.float32
            ).astype(jnp.bfloat16)
            at += 1
            if at % 8 == 0:
                done = pl.ds((at - 8) * HEAD, 8 * HEAD)
                copies.append(
                    pltpu.make_async_copy(
                        attended_ref.at[:, done], result_ref.at[:, done], sems.at[at // 8 - 1]
                    )
                )
                copies[-1].start()
    for copy in copies:
        copy.wait()


def attend(n_type, own, back, values, tile):
    slots, width = values.shape
    return pl.pallas_call(
        functools.partial(attend_kernel, n_type, len(own)),
        out_shape=jax.ShapeDtypeStruct((tile, width), jnp.bfloat16),
        in_specs=[VMEM] * (1 + 2 * len(own)),
        out_specs=pl.BlockSpec(memory_space=pl.ANY),
        scratch_shapes=[
            pltpu.VMEM((slots, width), jnp.bfloat16),
            pltpu.VMEM((tile, width), jnp.bfloat16),
            pltpu.SemaphoreType.DMA((width // HEAD // 8,)),
        ],
        compiler_params=params(8),
        cost_estimate=cost(0, 0),
    )(*held([values, *own, *back]))


def swap(x, axis, size, s):
    return lax.ppermute(x, axis, [(i, i ^ s) for i in range(size)])


def as_one_step(fn, *operands):
    shapes = jax.eval_shape(fn, *operands)
    blank = lambda *_: jax.tree.map(lambda x: jnp.zeros(x.shape, x.dtype), shapes)
    return lax.cond(lax.axis_index("type") >= 0, fn, blank, *operands)


def on_device(n_dp, n_type, tokens, token_types, tile_mask, queries, keys, gate_weight, up_weight, down_weight):
    tile, width = tokens.shape
    heads = width // HEAD
    tie = lax.optimization_barrier
    n_same = n_dp // 2
    outgoing = route(n_type, token_types.reshape(1, tile), tile_mask.reshape(1, n_type), tokens)
    incoming = [outgoing[0]] + [swap(outgoing[s], "type", n_type, s) for s in range(1, n_type)]

    def experts(incoming, *weights):
        packed, info = pack(n_type, incoming)
        weights = fetch(weights)
        rows = [packed]
        for p in range(1, n_same):
            low = p & -p
            rows.append(swap(rows[p - low], "dp", n_dp, 2 * low))
        rows, weights = tie((rows, weights))
        same_core = jnp.concatenate(rows, axis=0)
        return info, *ffn(same_core, swap(same_core, "dp", n_dp, 1), *weights)

    def gather_sum(own_rows, away_rows, *beside):
        chip_rows = own_rows + swap(away_rows, "dp", n_dp, 1).astype(jnp.float32)
        chip_rows = chip_rows.astype(jnp.bfloat16)
        pieces = [chip_rows[p * EXP_CAP : (p + 1) * EXP_CAP] for p in range(n_same)]
        pieces = [pieces[0]] + [swap(pieces[p], "dp", n_dp, 2 * p) for p in range(1, n_same)]
        begun = None
        if beside:
            info, queries, tiles = beside
            begun = weigh_begin(n_type, info, queries, 0, tiles, [0, 1, 3])
            pieces, begun = tie((pieces, begun))
        total = pieces[0].astype(jnp.float32)
        for piece in pieces[1:]:
            total = total + piece.astype(jnp.float32)
        return total.astype(jnp.bfloat16), begun

    def spread(rows, step=1):
        while step < n_type:
            rows = jnp.concatenate([rows, swap(rows, "type", n_type, step)], axis=0)
            step *= 2
        return rows

    weights = (gate_weight[0], up_weight[0], down_weight[0])
    if n_type == 4:
        to_middle = [(0, 1), (3, 2)]
        across = [(1, 2), (2, 1)]
        to_end = [(1, 0), (2, 3)]
        incoming, keys, queries = tie((incoming, keys, queries))
        near = lax.ppermute(keys, "type", to_middle)
        other = lax.ppermute(keys, "type", across)
        guest = lax.ppermute(queries, "type", to_middle)
        info, own_rows, away_rows = as_one_step(experts, incoming, *weights)
        own_rows, near = tie((own_rows, near))
        far = lax.ppermute(near, "type", across)
        tiles = [keys, near, other]
        expert_rows, (state, kept) = as_one_step(
            gather_sum, own_rows, away_rows, info, queries, tiles
        )
        twin = swap(expert_rows, "type", n_type, 1)
        expert_rows, guest = tie((expert_rows, guest))
        (guest_state,) = weigh_begin(n_type, info, guest, 1, tiles, [0, 1, 3])
        twin, guest_state, far = tie((twin, guest_state, far))
        values = spread(jnp.concatenate([expert_rows, twin], axis=0), 2)
        own_weights, back_weights = [], []
        ends = [0, heads]
        for first, last in zip(ends[:-1], ends[1:]):
            own, theirs = weigh_end(
                n_type,
                info,
                kept,
                far,
                [queries, guest],
                [state, guest_state],
                [0, 1, 3, 2],
                first,
                last - first,
                (1 << 30) if first > 0 else 0,
            )
            own_weights.append(own)
            back_weights.append(lax.ppermute(theirs, "type", to_end))
    else:
        info, own_rows, away_rows = experts(incoming, *weights)
        expert_rows, _ = gather_sum(own_rows, away_rows)
        values = spread(expert_rows)
        tiles = [keys] + [swap(keys, "type", n_type, s) for s in range(1, n_type)]
        ids = list(range(n_type))
        state, kept = weigh_begin(n_type, info, queries, 0, tiles[:-1], ids[:-1])
        own_weights = list(
            weigh_end(n_type, info, kept, tiles[-1], [queries], [state], ids, 0, heads)
        )
        back_weights = own_weights
    expert_out = expert_output(n_type, info, values, tile)
    values, expert_out = tie((values, expert_out))
    attended = attend(n_type, own_weights, back_weights, values, tile)
    return (expert_out, attended)


def solution(mesh):
    return jax.shard_map(
        functools.partial(on_device, mesh.shape["dp"], mesh.shape["type"]),
        mesh=mesh,
        in_specs=(
            P(("dp", "type"), None),
            P(("dp", "type"), None),
            P("dp", "type", None),
            P(("dp", "type"), None),
            P(("dp", "type"), None),
            P("type", None, "dp"),
            P("type", None, "dp"),
            P("type", "dp", None),
        ),
        out_specs=(P(("dp", "type"), None), P(("dp", "type"), None)),
        check_vma=False,
    )
```

```python
import functools
import math

import jax
import jax.numpy as jnp
from jax import lax
from jax.experimental import pallas as pl
from jax.experimental.pallas import tpu as pltpu
from jax.sharding import PartitionSpec as P

HEAD = 128
EXP_CAP = 16
LANES = 128
MASKED = -1e30
MIB = 1024 * 1024
VMEM = pl.BlockSpec(memory_space=pltpu.VMEM)


def params(mib, **more):
    return pltpu.CompilerParams(vmem_limit_bytes=mib * MIB, **more)


def held(arrays):
    return [pltpu.with_memory_space_constraint(x, pltpu.VMEM) for x in arrays]


def cost(flops, bytes_accessed, transcendentals=0):
    return pl.CostEstimate(
        flops=int(flops), bytes_accessed=int(bytes_accessed), transcendentals=int(transcendentals)
    )


def strict_upper(size):
    earlier = lax.broadcasted_iota(jnp.int32, (size, size), 0)
    later = lax.broadcasted_iota(jnp.int32, (size, size), 1)
    return (earlier < later).astype(jnp.bfloat16)


def columns(width):
    for chunk in (1024, 512, 256, 128):
        if width % chunk == 0:
            return chunk, width // chunk
    raise ValueError(width)


def route_kernel(n_type, types_ref, mask_ref, tokens_ref, *refs):
    out_refs, select_ref = refs[:n_type], refs[n_type]
    me = lax.axis_index("type")
    step = pl.program_id(0)
    rows, chunk = tokens_ref.shape
    width = out_refs[0].shape[1] - LANES

    @pl.when(step == 0)
    def _():
        types = types_ref[...]
        hot = lax.broadcasted_iota(jnp.int32, (EXP_CAP, rows), 0) == types
        before = jnp.dot(
            hot.astype(jnp.bfloat16), strict_upper(rows), preferred_element_type=jnp.float32
        )
        rank = jnp.sum(jnp.where(hot, before, 0.0), axis=0, keepdims=True).astype(jnp.int32)
        place = jnp.where(rank < EXP_CAP, jnp.bitwise_xor(types, me) * EXP_CAP + rank, -1)
        select_ref[...] = (
            lax.broadcasted_iota(jnp.int32, (n_type * EXP_CAP, rows), 0) == place
        ).astype(jnp.bfloat16)
        lane = lax.broadcasted_iota(jnp.int32, (EXP_CAP, LANES), 1)
        row = lax.broadcasted_iota(jnp.int32, (EXP_CAP, LANES), 0)
        mask_row = jnp.zeros((EXP_CAP, LANES), jnp.int32)
        for j in range(n_type):
            mask_row = jnp.where(lane == j, mask_ref[0, j], mask_row)
        extra = jnp.where(row == 0, types, jnp.where(row == 1, mask_row, 0))
        extra = extra.astype(jnp.float32).astype(jnp.bfloat16)
        for s in range(n_type):
            out_refs[s][:, pl.ds(width, LANES)] = extra

    moved = jnp.dot(select_ref[...], tokens_ref[...], preferred_element_type=jnp.float32).astype(
        jnp.bfloat16
    )
    span = pl.ds(pl.multiple_of(step * chunk, chunk), chunk)
    for s in range(n_type):
        out_refs[s][:, span] = moved[s * EXP_CAP : (s + 1) * EXP_CAP]


def route(n_type, types, mask_row, tokens):
    rows, width = tokens.shape
    wide = width + LANES
    chunk, count = width // 2, 2
    return pl.pallas_call(
        functools.partial(route_kernel, n_type),
        grid=(count,),
        out_shape=[jax.ShapeDtypeStruct((EXP_CAP, wide), jnp.bfloat16)] * n_type,
        in_specs=[
            VMEM,
            pl.BlockSpec(memory_space=pltpu.SMEM),
            pl.BlockSpec((rows, chunk), lambda i: (0, i)),
        ],
        out_specs=[VMEM] * n_type,
        scratch_shapes=[pltpu.VMEM((n_type * EXP_CAP, rows), jnp.bfloat16)],
        compiler_params=params(8, dimension_semantics=("arbitrary",)),
        cost_estimate=cost(0, 0),
    )(*[pltpu.with_memory_space_constraint(x, pltpu.HBM) for x in (types, mask_row, tokens)])


def fetch_kernel(count, *refs):
    sems = refs[2 * count]
    copies = [pltpu.make_async_copy(refs[i], refs[count + i], sems.at[i]) for i in range(count)]
    for copy in copies:
        copy.start()
    for copy in copies:
        copy.wait()


def fetch(arrays):
    count = len(arrays)
    return pl.pallas_call(
        functools.partial(fetch_kernel, count),
        out_shape=[pltpu.VMEM(x.shape, x.dtype) for x in arrays],
        in_specs=[pl.BlockSpec(memory_space=pl.ANY)] * count,
        out_specs=[VMEM] * count,
        scratch_shapes=[pltpu.SemaphoreType.DMA((count,))],
        compiler_params=params(1),
        cost_estimate=cost(0, 2 * sum(x.size * 2 for x in arrays)),
    )(*[pltpu.with_memory_space_constraint(x, pltpu.HBM) for x in arrays])


def pack_kernel(n_type, *refs):
    in_refs, packed_ref, info_ref = refs[:n_type], refs[n_type], refs[n_type + 1]
    me = lax.axis_index("type")
    width = packed_ref.shape[1]
    tail = pl.ds(width, LANES)
    type_rows = 2 * 8
    row = lax.broadcasted_iota(jnp.int32, (type_rows, LANES), 0)
    upper = strict_upper(LANES)
    extras = [ref[:, tail].astype(jnp.float32) for ref in in_refs]
    types = [e[0:1] for e in extras]
    hots = [row == t.astype(jnp.int32) for t in types]
    befores = [
        jnp.dot(h.astype(jnp.bfloat16), upper, preferred_element_type=jnp.float32) for h in hots
    ]
    counts = [jnp.sum(h.astype(jnp.float32), axis=1, keepdims=True) for h in hots]
    lane16 = lax.broadcasted_iota(jnp.int32, (EXP_CAP, n_type * EXP_CAP), 1)
    slot16 = lax.broadcasted_iota(jnp.int32, (EXP_CAP, n_type * EXP_CAP), 0)
    compact = jnp.zeros((EXP_CAP, n_type * EXP_CAP), jnp.bool_)
    mine = lax.broadcasted_iota(jnp.int32, (type_rows, 1), 0) == me
    info_rows = []
    for s in range(n_type):
        ahead = jnp.zeros((type_rows, 1), jnp.float32)
        for other in range(n_type):
            if other != s:
                first = jnp.bitwise_xor(me, other) < jnp.bitwise_xor(me, s)
                ahead = ahead + jnp.where(first, counts[other], 0.0)
        rank = jnp.sum(jnp.where(hots[s], befores[s] + ahead, 0.0), axis=0, keepdims=True)
        info_rows.append(jnp.where(rank < EXP_CAP, types[s] * EXP_CAP + rank, -1.0))
        offset = jnp.sum(jnp.where(mine, ahead, 0.0)).astype(jnp.int32)
        amount = jnp.sum(jnp.where(mine, counts[s], 0.0)).astype(jnp.int32)
        local = lane16 - s * EXP_CAP
        compact = compact | (
            (local >= 0) & (local < EXP_CAP) & (local < amount) & (local + offset == slot16)
        )
    lane = lax.broadcasted_iota(jnp.int32, (1, LANES), 1)
    for q in range(2):
        for s in range(n_type):
            kept = jnp.sum(
                jnp.where(lane == jnp.bitwise_xor(me, s), extras[q][1:2], 0.0),
                axis=1,
                keepdims=True,
            )
            info_rows.append(jnp.broadcast_to(jnp.where(kept == 1.0, 0.0, MASKED), (1, LANES)))
    for at, info_row in enumerate(info_rows):
        info_ref[at : at + 1, :] = info_row
    compact = compact.astype(jnp.bfloat16)
    chunk, count = columns(width)
    for c in range(count):
        span = pl.ds(c * chunk, chunk)
        rows = jnp.concatenate([ref[:, span] for ref in in_refs], axis=0)
        packed_ref[:, span] = jnp.dot(compact, rows, preferred_element_type=jnp.float32).astype(
            jnp.bfloat16
        )


def pack(n_type, incoming):
    width = incoming[0].shape[1] - LANES
    return pl.pallas_call(
        functools.partial(pack_kernel, n_type),
        out_shape=[
            jax.ShapeDtypeStruct((EXP_CAP, width), jnp.bfloat16),
            jax.ShapeDtypeStruct((3 * n_type, LANES), jnp.float32),
        ],
        in_specs=[VMEM] * n_type,
        out_specs=[VMEM, VMEM],
        compiler_params=params(8),
        cost_estimate=cost(0, 0),
    )(*held(incoming))


def ffn_kernel(near_ref, far_ref, gate_ref, up_ref, down_ref, own_ref, away_ref, x_ref, hidden_ref):
    half = near_ref.shape[0]
    x_ref[:half] = near_ref[...]
    x_ref[half:] = far_ref[...]
    hidden = gate_ref.shape[1]
    for at in range(0, hidden, 256):
        span = pl.ds(at, min(256, hidden - at))
        gate = jnp.dot(x_ref[...], gate_ref[:, span], preferred_element_type=jnp.float32)
        up = jnp.dot(x_ref[...], up_ref[:, span], preferred_element_type=jnp.float32)
        hidden_ref[:, span] = (gate / (1.0 + jnp.exp(-gate)) * up).astype(jnp.bfloat16)
    for at in range(0, down_ref.shape[1], 512):
        span = pl.ds(at, 512)
        out = jnp.dot(hidden_ref[...], down_ref[:, span], preferred_element_type=jnp.float32)
        own_ref[:, span] = out[:half]
        away_ref[:, span] = out[half:].astype(jnp.bfloat16)


def ffn(near, far, gate, up, down):
    half, width = near.shape
    rows = 2 * half
    hidden = gate.shape[1]
    return pl.pallas_call(
        ffn_kernel,
        out_shape=[
            jax.ShapeDtypeStruct((half, width), jnp.float32),
            jax.ShapeDtypeStruct((half, width), jnp.bfloat16),
        ],
        in_specs=[VMEM] * 5,
        out_specs=[VMEM] * 2,
        scratch_shapes=[
            pltpu.VMEM((rows, width), jnp.bfloat16),
            pltpu.VMEM((rows, hidden), jnp.bfloat16),
        ],
        compiler_params=params(16),
        cost_estimate=cost(0, 0),
    )(*held([near, far, gate, up, down]))


FACTOR = math.log2(math.e) / math.sqrt(HEAD)


def slots_of(slots, tile, s, info_ref):
    row = lax.broadcasted_iota(jnp.int32, (slots, tile), 0)
    return row == info_ref[s : s + 1, :].astype(jnp.int32)


def mask_row(n_type, q, s, info_ref):
    line = (1 + q) * n_type + s
    return info_ref[line : line + 1, :]


def product(rows, queries):
    return lax.dot_general(
        rows, queries, (((1,), (1,)), ((), ())), preferred_element_type=jnp.float32
    )


def pair_of(query):
    lane = lax.broadcasted_iota(jnp.int32, query.shape, 1)
    zero = jnp.zeros_like(query)
    return jnp.concatenate(
        [jnp.where(lane < HEAD, query, zero), jnp.where(lane >= HEAD, query, zero)], axis=0
    )


def pair_scores(n_type, q, tile_ids, info_ref, key_refs, query_ref, span):
    tile = query_ref.shape[0]
    scores = product(
        jnp.concatenate([ref[:, span] for ref in key_refs], axis=0), pair_of(query_ref[:, span])
    )
    scores = [scores[i * tile : (i + 1) * tile] for i in range(len(tile_ids))]
    masks = [mask_row(n_type, q, s, info_ref) for s in tile_ids]
    return [x + jnp.concatenate([m, m], axis=1) for x, m in zip(scores, masks)]


def top_of(scores):
    return functools.reduce(jnp.maximum, [jnp.max(x, axis=0, keepdims=True) for x in scores])


def total_of(scores, top):
    return sum(jnp.sum(jnp.exp2((x - top) * FACTOR), axis=0, keepdims=True) for x in scores)


def in_middle(body, n_type, *args):
    me = lax.axis_index("type")
    step = pl.program_id(0)
    if n_type != 4:
        body(step, n_type, *args)
    else:

        @pl.when((me > 0) & (me < n_type - 1))
        def _():
            body(step, n_type, *args)


def weigh_begin_body(step, n_type, tile_ids, query_id, info_ref, query_ref, *refs):
    key_refs = refs[: len(tile_ids)]
    state_ref, *kept_refs = refs[len(tile_ids) :]
    tile, width = query_ref.shape
    for kept_ref in kept_refs:
        slots = kept_ref.shape[0]
        select = [slots_of(slots, tile, s, info_ref).astype(jnp.bfloat16) for s in tile_ids]
        kept_ref[...] = jnp.dot(
            jnp.concatenate(select, axis=1),
            jnp.concatenate([ref[...] for ref in key_refs], axis=0),
            preferred_element_type=jnp.float32,
        ).astype(jnp.bfloat16)
    for at in range(0, width, 2 * HEAD):
        span = pl.ds(at, 2 * HEAD)
        scores = pair_scores(n_type, query_id, tile_ids, info_ref, key_refs, query_ref, span)
        top = top_of(scores)
        total = total_of(scores, top)
        for i in range(2):
            mine = slice(i * tile, (i + 1) * tile)
            head = at // HEAD + i
            state_ref[head, :8] = jnp.broadcast_to(total[:, mine], (8, tile))
            state_ref[head, 8:] = jnp.broadcast_to(top[:, mine], (8, tile))


PER_STEP = 16


def weigh_begin(n_type, info, query, query_id, keys, tile_ids):
    tile, width = query.shape
    heads = width // HEAD
    slots = n_type * EXP_CAP
    block = pl.BlockSpec((tile, PER_STEP * HEAD), lambda i: (0, i))
    return pl.pallas_call(
        functools.partial(in_middle, weigh_begin_body, n_type, tile_ids, query_id),
        grid=(heads // PER_STEP,),
        out_shape=[
            jax.ShapeDtypeStruct((heads, 2 * 8, tile), jnp.float32),
            jax.ShapeDtypeStruct((slots, width), jnp.bfloat16),
        ][: 2 - query_id],
        in_specs=[VMEM] + [block] * (1 + len(keys)),
        out_specs=[
            pl.BlockSpec((PER_STEP, 2 * 8, tile), lambda i: (i, 0, 0)),
            pl.BlockSpec((slots, PER_STEP * HEAD), lambda i: (0, i)),
        ][: 2 - query_id],
        compiler_params=params(16, dimension_semantics=("arbitrary",)),
        cost_estimate=cost(0, 16 * tile * tile * heads),
    )(info, query, *keys)


def weigh_end_body(step, n_type, tile_ids, info_ref, kept_ref, last_ref, *refs):
    n_query = (len(refs) - 1) // 3
    query_refs, state_refs = refs[:n_query], refs[n_query : 2 * n_query]
    out_refs, bias_ref = refs[2 * n_query : 3 * n_query], refs[3 * n_query]
    slots, width = kept_ref.shape
    tile = last_ref.shape[0]

    @pl.when(step == 0)
    def _():
        bias = [jnp.full((slots, tile), MASKED, jnp.float32) for _ in range(n_query)]
        for s in tile_ids:
            chosen = slots_of(slots, tile, s, info_ref).astype(jnp.float32)
            filled = jnp.max(chosen, axis=1, keepdims=True)
            for q in range(n_query):
                bias[q] = jnp.where(filled > 0.0, mask_row(n_type, q, s, info_ref), bias[q])
        for q in range(n_query):
            bias_ref[:, q * tile : (q + 1) * tile] = bias[q]

    select = slots_of(slots, tile, tile_ids[-1], info_ref).astype(jnp.bfloat16)
    found = jnp.dot(select, last_ref[...], preferred_element_type=jnp.float32)
    kept = (kept_ref[...].astype(jnp.float32) + found).astype(jnp.bfloat16)
    last_mask = jnp.concatenate(
        [mask_row(n_type, q, tile_ids[-1], info_ref) for q in range(n_query)], axis=1
    )
    for head in range(width // HEAD):
        span = slice(head * HEAD, (head + 1) * HEAD)
        scores = product(
            jnp.concatenate([last_ref[:, span], kept[:, span]], axis=0),
            jnp.concatenate([ref[:, span] for ref in query_refs], axis=0),
        )
        last = scores[:tile] + last_mask
        before = jnp.concatenate([ref[head, 8:9] for ref in state_refs], axis=1)
        begun = jnp.concatenate([ref[head, 0:1] for ref in state_refs], axis=1)
        top = jnp.maximum(before, jnp.max(last, axis=0, keepdims=True))
        total = total_of([last], top) + begun * jnp.exp2((before - top) * FACTOR)
        weights = jnp.exp2((scores[tile:] + bias_ref[...] - top) * FACTOR) * (1.0 / total)
        for q in range(n_query):
            out_refs[q][head] = weights[:, q * tile : (q + 1) * tile].astype(jnp.bfloat16)


def weigh_end(n_type, info, kept, last_key, queries, states, tile_ids, first_head, heads, weight=0):
    tile = last_key.shape[0]
    n_query = len(queries)
    slots = n_type * EXP_CAP
    first = first_head // PER_STEP
    block = pl.BlockSpec((tile, PER_STEP * HEAD), lambda i: (0, i + first))
    state_block = pl.BlockSpec((PER_STEP, 2 * 8, tile), lambda i: (i + first, 0, 0))
    out_block = pl.BlockSpec((PER_STEP, slots, tile), lambda i: (i, 0, 0))
    return pl.pallas_call(
        functools.partial(in_middle, weigh_end_body, n_type, tile_ids),
        grid=(heads // PER_STEP,),
        out_shape=[jax.ShapeDtypeStruct((heads, slots, tile), jnp.bfloat16)] * n_query,
        in_specs=[VMEM, pl.BlockSpec((slots, PER_STEP * HEAD), lambda i: (0, i + first))]
        + [block] * (1 + n_query)
        + [state_block] * n_query,
        out_specs=[out_block] * n_query,
        scratch_shapes=[pltpu.VMEM((slots, n_query * tile), jnp.float32)],
        compiler_params=params(16, dimension_semantics=("arbitrary",)),
        cost_estimate=cost(0, weight),
    )(info, kept, last_key, *queries, *states)


def by_expert(n_type, values_ref, value_ref):
    me = lax.axis_index("type")
    for s in range(n_type):
        at = pl.multiple_of(jnp.bitwise_xor(me, s) * EXP_CAP, EXP_CAP)
        value_ref[pl.ds(at, EXP_CAP), :] = values_ref[s * EXP_CAP : (s + 1) * EXP_CAP]


CONTRACT = (((0,), (0,)), ((), ()))


def expert_out_kernel(n_type, info_ref, values_ref, out_ref, value_ref):
    tile, width = out_ref.shape
    by_expert(n_type, values_ref, value_ref)
    select = slots_of(n_type * EXP_CAP, tile, 0, info_ref).astype(jnp.bfloat16)
    chunk, count = columns(width)
    for c in range(count):
        span = pl.ds(c * chunk, chunk)
        out_ref[:, span] = lax.dot_general(
            select, value_ref[:, span], CONTRACT, preferred_element_type=jnp.float32
        ).astype(jnp.bfloat16)


def expert_output(n_type, info, values, tile):
    slots, width = values.shape
    return pl.pallas_call(
        functools.partial(expert_out_kernel, n_type),
        out_shape=jax.ShapeDtypeStruct((tile, width), jnp.bfloat16),
        in_specs=[VMEM] * 2,
        out_specs=VMEM,
        scratch_shapes=[pltpu.VMEM((slots, width), jnp.bfloat16)],
        compiler_params=params(8),
        cost_estimate=cost(0, 0),
    )(*held([info, values]))


def attend_kernel(n_type, n_part, values_ref, *refs):
    own_refs, back_refs = refs[:n_part], refs[n_part : 2 * n_part]
    result_ref, value_ref, attended_ref, sems = refs[2 * n_part :]
    me = lax.axis_index("type")
    ends = (me == 0) | (me == n_type - 1)
    by_expert(n_type, values_ref, value_ref)
    at = 0
    copies = []
    for part in range(n_part):
        for h in range(own_refs[part].shape[0]):
            span = pl.ds(at * HEAD, HEAD)
            weights = jnp.where(ends, back_refs[part][h], own_refs[part][h])
            attended_ref[:, span] = lax.dot_general(
                weights, value_ref[:, span], CONTRACT, preferred_element_type=jnp.float32
            ).astype(jnp.bfloat16)
            at += 1
            if at % 4 == 0:
                done = pl.ds((at - 4) * HEAD, 4 * HEAD)
                copies.append(
                    pltpu.make_async_copy(
                        attended_ref.at[:, done], result_ref.at[:, done], sems.at[at // 4 - 1]
                    )
                )
                copies[-1].start()
    for copy in copies:
        copy.wait()


def attend(n_type, own, back, values, tile):
    slots, width = values.shape
    return pl.pallas_call(
        functools.partial(attend_kernel, n_type, len(own)),
        out_shape=jax.ShapeDtypeStruct((tile, width), jnp.bfloat16),
        in_specs=[VMEM] * (1 + 2 * len(own)),
        out_specs=pl.BlockSpec(memory_space=pl.ANY),
        scratch_shapes=[
            pltpu.VMEM((slots, width), jnp.bfloat16),
            pltpu.VMEM((tile, width), jnp.bfloat16),
            pltpu.SemaphoreType.DMA((width // HEAD // 4,)),
        ],
        compiler_params=params(8),
        cost_estimate=cost(0, 0),
    )(*held([values, *own, *back]))


def swap(x, axis, size, s):
    return lax.ppermute(x, axis, [(i, i ^ s) for i in range(size)])


def as_one_step(fn, *operands):
    shapes = jax.eval_shape(fn, *operands)
    blank = lambda *_: jax.tree.map(lambda x: jnp.zeros(x.shape, x.dtype), shapes)
    return lax.cond(lax.axis_index("type") >= 0, fn, blank, *operands)


def on_device(n_dp, n_type, tokens, token_types, tile_mask, queries, keys, gate_weight, up_weight, down_weight):
    tile, width = tokens.shape
    heads = width // HEAD
    tie = lax.optimization_barrier
    n_same = n_dp // 2
    outgoing = route(n_type, token_types.reshape(1, tile), tile_mask.reshape(1, n_type), tokens)
    incoming = [outgoing[0]] + [swap(outgoing[s], "type", n_type, s) for s in range(1, n_type)]

    def experts(incoming, *weights):
        packed, info = pack(n_type, incoming)
        weights = fetch(weights)
        rows = [packed]
        for p in range(1, n_same):
            low = p & -p
            rows.append(swap(rows[p - low], "dp", n_dp, 2 * low))
        rows, weights = tie((rows, weights))
        same_core = jnp.concatenate(rows, axis=0)
        return info, *ffn(same_core, swap(same_core, "dp", n_dp, 1), *weights)

    def gather_sum(own_rows, away_rows, *beside):
        chip_rows = own_rows + swap(away_rows, "dp", n_dp, 1).astype(jnp.float32)
        chip_rows = chip_rows.astype(jnp.bfloat16)
        pieces = [chip_rows[p * EXP_CAP : (p + 1) * EXP_CAP] for p in range(n_same)]
        pieces = [pieces[0]] + [swap(pieces[p], "dp", n_dp, 2 * p) for p in range(1, n_same)]
        begun = None
        if beside:
            info, queries, tiles = beside
            begun = weigh_begin(n_type, info, queries, 0, tiles, [0, 1, 3])
            pieces, begun = tie((pieces, begun))
        total = pieces[0].astype(jnp.float32)
        for piece in pieces[1:]:
            total = total + piece.astype(jnp.float32)
        return total.astype(jnp.bfloat16), begun

    def spread(rows, step=1):
        while step < n_type:
            rows = jnp.concatenate([rows, swap(rows, "type", n_type, step)], axis=0)
            step *= 2
        return rows

    weights = (gate_weight[0], up_weight[0], down_weight[0])
    if n_type == 4:
        to_middle = [(0, 1), (3, 2)]
        across = [(1, 2), (2, 1)]
        to_end = [(1, 0), (2, 3)]
        incoming, keys, queries = tie((incoming, keys, queries))
        near = lax.ppermute(keys, "type", to_middle)
        other = lax.ppermute(keys, "type", across)
        guest = lax.ppermute(queries, "type", to_middle)
        info, own_rows, away_rows = as_one_step(experts, incoming, *weights)
        own_rows, near = tie((own_rows, near))
        far = lax.ppermute(near, "type", across)
        tiles = [keys, near, other]
        expert_rows, (state, kept) = as_one_step(
            gather_sum, own_rows, away_rows, info, queries, tiles
        )
        twin = swap(expert_rows, "type", n_type, 1)
        expert_rows, guest = tie((expert_rows, guest))
        (guest_state,) = weigh_begin(n_type, info, guest, 1, tiles, [0, 1, 3])
        twin, guest_state, far = tie((twin, guest_state, far))
        values = spread(jnp.concatenate([expert_rows, twin], axis=0), 2)
        own_weights, back_weights = [], []
        ends = [0, heads]
        for first, last in zip(ends[:-1], ends[1:]):
            own, theirs = weigh_end(
                n_type,
                info,
                kept,
                far,
                [queries, guest],
                [state, guest_state],
                [0, 1, 3, 2],
                first,
                last - first,
                (1 << 30) if first > 0 else 0,
            )
            own_weights.append(own)
            back_weights.append(lax.ppermute(theirs, "type", to_end))
    else:
        info, own_rows, away_rows = experts(incoming, *weights)
        expert_rows, _ = gather_sum(own_rows, away_rows)
        values = spread(expert_rows)
        tiles = [keys] + [swap(keys, "type", n_type, s) for s in range(1, n_type)]
        ids = list(range(n_type))
        state, kept = weigh_begin(n_type, info, queries, 0, tiles[:-1], ids[:-1])
        own_weights = list(
            weigh_end(n_type, info, kept, tiles[-1], [queries], [state], ids, 0, heads)
        )
        back_weights = own_weights
    expert_out = expert_output(n_type, info, values, tile)
    values, expert_out = tie((values, expert_out))
    attended = attend(n_type, own_weights, back_weights, values, tile)
    return (expert_out, attended)


def solution(mesh):
    return jax.shard_map(
        functools.partial(on_device, mesh.shape["dp"], mesh.shape["type"]),
        mesh=mesh,
        in_specs=(
            P(("dp", "type"), None),
            P(("dp", "type"), None),
            P("dp", "type", None),
            P(("dp", "type"), None),
            P(("dp", "type"), None),
            P("type", None, "dp"),
            P("type", None, "dp"),
            P("type", "dp", None),
        ),
        out_specs=(P(("dp", "type"), None), P(("dp", "type"), None)),
        check_vma=False,
    )
```
